32 devices in a mesh: pair: 4 (over z), aux: 8 (over y, x, core).
Axes of the slice: x: 2, y: 2, z: 4, core: 2. Of those that a mesh axis runs over, the one named last changes fastest.
Arguments:
- integrals: float32 [24, 128, 16, 128], P('pair', 'aux'), may hold values from -0.0034179688 to 0.0034179688
- mu_list: int32 [8, 24], P('aux', 'pair'), may hold values from 0 to 63, as said below
- lam_list: int32 [8, 24, 8], P('aux', 'pair'), may hold values from 0 to 63, as said below
- coeffs: float32 [64, 16, 64], replicated, may hold values from -6 to 6
- block_size: int32 [64], replicated, may hold values from 9 to 16
- block_order: int32 [64], replicated, may hold values from 0 to 63, as said below
Outputs:
- exchange: float32 [1024, 1024], P('pair', 'aux')
The draws below stay inside these ranges and needn't reach their ends.
Inputs may be any that keep to these rules, and one draw needn't show every extreme that they name: `mu_list`: for every auxiliary index and every pair index, the 6 tiles of that device name row blocks whose owner pair index (block_order // 16) is shared by at most 2 of them, and some owner is named by exactly 2. `lam_list`: the 8 partner blocks of one tile are distinct. `block_order`: A permutation of the atom blocks.
All inputs are finite; a program needn't handle non-finite values.
Results may differ from the reference program's by a relative error of at most 0.0013.
Values may be sent and summed in bfloat16 or wider, within the bound.
A program may use at most 64 MiB of HBM per device.

```python
import jax
import jax.numpy as jnp
from jax import lax

BS = 16
NOCC = 64
LAM = 8
CAP = 2
AUX_DEV = 16
BLK_DEV = 16
TILES = 6
NBLK = 64
AUX = 128
N_PAIR = 4
N_AUX = 8


def shared_order(key):
    return jax.random.permutation(jax.random.fold_in(key, 101), NBLK).astype(jnp.int32)


def draw_block_order(key, part):
    return shared_order(key)


def draw_mu_list(key, part):
    order = shared_order(key)
    key = jax.random.fold_in(key, 3)
    inverse = jnp.zeros((NBLK,), jnp.int32).at[order].set(jnp.arange(NBLK, dtype=jnp.int32))
    first, second = jax.random.split(key)
    keys = jax.random.split(first, N_AUX * N_PAIR)
    slots = jax.vmap(lambda k: jax.random.permutation(k, N_PAIR * CAP))(keys)[:, :TILES].astype(jnp.int32)
    owner = slots // CAP
    within = jax.random.randint(second, owner.shape, 0, BLK_DEV).astype(jnp.int32)
    blocks = inverse[owner * BLK_DEV + within]
    return blocks.reshape(N_AUX, N_PAIR * TILES)


def draw_lam_list(key, part):
    key = jax.random.fold_in(key, 5)
    keys = jax.random.split(key, N_AUX * N_PAIR * TILES)
    chosen = jax.vmap(lambda k: jax.random.permutation(k, NBLK)[:LAM])(keys).astype(jnp.int32)
    return chosen.reshape(N_AUX, N_PAIR * TILES, LAM)


def touch_ends(entries, stream_key, least, high):
    spot = [jax.random.randint(jax.random.fold_in(stream_key, axis), (), 0, length) for axis, length in enumerate(entries.shape)]
    main_axis = entries.shape.index(max(entries.shape))
    neighbour = spot[:main_axis] + [(spot[main_axis] + 1) % entries.shape[main_axis]] + spot[main_axis + 1:]
    return entries.at[tuple(spot)].set(least).at[tuple(neighbour)].set(high)


def block_scale(stream_key, extent, shards, smallest, top_value):
    loudness = 1.0
    for dim, blocks in shards:
        draws = jax.random.uniform(jax.random.fold_in(jax.random.fold_in(stream_key, 6), dim), (blocks,), jnp.float32, smallest / len(shards), top_value / len(shards))
        loudness = loudness * jnp.repeat(jnp.exp(draws), extent[dim] // blocks).reshape((-1,) + (1,) * (len(extent) - 1 - dim))
    return loudness


def scatter_about(own_key, extent, spread, reach, shards=(), kind=jnp.bfloat16):
    drawn = spread * jax.random.normal(own_key, extent, jnp.float32)
    if shards:
        drawn = drawn * block_scale(own_key, extent, shards, -0.22, 0.18)
    return jnp.clip(drawn, -reach, reach).astype(kind)


def setup_inputs(seed: int = 0) -> dict:
    key_list = jax.random.split(jax.random.key(seed), 7)
    return {
        "integrals": scatter_about(key_list[0], (N_PAIR * TILES, AUX, BS, LAM * BS), (3 * LAM * BS * AUX * NOCC) ** -0.5, 0.0034179688, ((0, 4), (1, 8)), jnp.float32),
        "mu_list": draw_mu_list(jax.random.fold_in(key_list[6], 71), 0),
        "lam_list": draw_lam_list(jax.random.fold_in(key_list[6], 71), 0),
        "coeffs": scatter_about(key_list[3], (NBLK, BS, NOCC), 1.0, 6.0, (), jnp.float32),
        "block_size": touch_ends(jax.random.randint(key_list[4], (NBLK,), 9, BS + 1), jax.random.fold_in(key_list[4], 1), 9, BS).astype(jnp.int32),
        "block_order": draw_block_order(jax.random.fold_in(key_list[6], 71), 0),
    }


def reference(integrals, mu_list, lam_list, coeffs, block_size, block_order):
    nblk, width, nocc = coeffs.shape
    live = (jnp.arange(width, dtype=jnp.int32)[None, :] < block_size[:, None]).astype(jnp.float32)
    masked = coeffs * live[:, :, None]
    tiles_all = integrals.shape[0]

    def one_block(index):
        start = (index * AUX_DEV).astype(jnp.int32)
        slab = lax.dynamic_slice_in_dim(integrals, start, AUX_DEV, 1)
        picked = masked[lam_list[index]].reshape(tiles_all, LAM * width, nocc)
        half = jnp.einsum("tqmk,tki->tmqi", slab, picked, precision=lax.Precision.HIGHEST).astype(jnp.bfloat16)
        place = block_order[mu_list[index]]
        select = (jnp.arange(nblk, dtype=jnp.int32)[:, None] == place[None, :]).astype(jnp.float32)
        summed = jnp.einsum("pt,tmqi->pmqi", select, half.astype(jnp.float32), precision=lax.Precision.HIGHEST)
        return summed.astype(jnp.bfloat16)

    stacked = lax.map(one_block, jnp.arange(N_AUX, dtype=jnp.int32))
    fitted = jnp.transpose(stacked, (1, 2, 0, 3, 4)).reshape(nblk * width, -1).astype(jnp.float32)
    product = jnp.dot(fitted, fitted.T, precision=lax.Precision.HIGHEST, preferred_element_type=jnp.float32)
    posmat = (block_order[None, :] == jnp.arange(nblk, dtype=jnp.int32)[:, None]).astype(jnp.float32)
    live_pos = jnp.dot(posmat, live, precision=lax.Precision.HIGHEST).reshape(-1)
    return product * live_pos[:, None] * live_pos[None, :]
```

```python
import functools

import jax
import jax.numpy as jnp
from jax import lax
from jax.experimental import pallas as pl
from jax.experimental.pallas import tpu as pltpu
from jax.sharding import PartitionSpec as P

CAP = 2
LANES = 128
LABEL_ROWS = 8
MESH = pl.DeviceIdType.MESH


def crossed(left, right):
    return lax.dot_general(
        left, right, (((1,), (1,)), ((), ())), preferred_element_type=jnp.float32
    )


def body(integrals, mu_list, lam_list, coeffs, block_size, block_order):
    tiles = integrals.shape[0]
    aux_rows = integrals.shape[1]
    width = integrals.shape[2]
    nblk, _, nocc = coeffs.shape
    npair = lax.axis_size("pair")
    here = lax.axis_index("pair")
    blk_dev = nblk // npair
    ao_dev = blk_dev * width
    slot_count = npair * CAP
    span = jnp.arange(width, dtype=jnp.int32)
    live = (span[None, :] < block_size[:, None]).astype(jnp.float32)
    masked = coeffs * live[:, :, None]
    picked = masked[lam_list[0]].reshape(tiles, -1, nocc)
    half = jnp.einsum("tqmk,tki->tmqi", integrals, picked, precision=lax.Precision.HIGHEST)
    half = half.astype(jnp.bfloat16).reshape(tiles, width * aux_rows * nocc)
    place = block_order[mu_list[0]]
    owner = place // blk_dev
    local = place % blk_dev
    order_ids = jnp.arange(tiles, dtype=jnp.int32)
    earlier = (owner[None, :] == owner[:, None]) & (order_ids[None, :] < order_ids[:, None])
    rank = jnp.sum(earlier.astype(jnp.int32), axis=1)
    slot = owner * CAP + rank
    select = jnp.arange(slot_count, dtype=jnp.int32)[:, None] == slot[None, :]
    outgoing = jnp.dot(
        select.astype(jnp.bfloat16), half, preferred_element_type=jnp.float32
    ).astype(jnp.bfloat16)
    outgoing = outgoing.reshape(npair, CAP, width * aux_rows * nocc)
    labels = jnp.sum(jnp.where(select, local[None, :] + 1, 0), axis=1) - 1
    labels = labels.reshape(npair, CAP)
    incoming, labels_in = (
        lax.all_to_all(outgoing, "pair", split_axis=0, concat_axis=0, tiled=True),
        lax.all_to_all(labels, "pair", split_axis=0, concat_axis=0, tiled=True),
    )
    assign = (
        labels_in.reshape(-1)[None, :] == jnp.arange(blk_dev, dtype=jnp.int32)[:, None]
    ).astype(jnp.bfloat16)
    fitted = jnp.dot(assign, incoming.reshape(slot_count, -1), preferred_element_type=jnp.float32)
    fitted = fitted.astype(jnp.bfloat16).reshape(ao_dev, aux_rows * nocc)
    partial_value = crossed(fitted, lax.all_gather(fitted, "pair", axis=0, tiled=True))
    summed = lax.psum_scatter(partial_value, "aux", scatter_dimension=1, tiled=True)
    posmat = (block_order[None, :] == jnp.arange(nblk, dtype=jnp.int32)[:, None]).astype(
        jnp.float32
    )
    live_pos = jnp.dot(posmat, live, precision=lax.Precision.HIGHEST).reshape(-1)
    cols = summed.shape[1]
    row_mask = lax.dynamic_slice_in_dim(live_pos, here * ao_dev, ao_dev, 0)
    col_mask = lax.dynamic_slice_in_dim(live_pos, lax.axis_index("aux") * cols, cols, 0)
    return summed * row_mask[:, None] * col_mask[None, :]


def mirrored(index, offset):
    result = index
    bit = 1
    while bit <= offset:
        if offset & bit:
            result = result + bit * (1 - 2 * ((index // bit) % 2))
        bit *= 2
    return result


def exchange_kernel(
    npair, naux, mu_ref, lam_ref, size_ref, order_ref, integrals_ref, coeffs_ref, out_ref,
    held, meta, sent, arrived, out_left, out_right, in_sem, meta_left, meta_right, meta_in, sum_out, sum_in,
):
    tiles, aux_rows, width, depth = integrals_ref.shape
    nocc = coeffs_ref.shape[2]
    partners = depth // width
    ao_dev, cols = out_ref.shape
    rows = tiles * width
    padded = held.shape[1]
    chunk = rows // 2
    slot_rows = npair * CAP * width
    here = lax.axis_index("pair")
    column = lax.axis_index("aux")

    barrier = pltpu.get_barrier_semaphore()

    def greet(device):
        pl.semaphore_signal(barrier, inc=1, device_id=device, device_id_type=MESH)

    for offset in range(1, naux):
        greet({"aux": mirrored(column, offset)})

    @pl.when(here > 0)
    def _():
        greet({"pair": here - 1})

    @pl.when(here < npair - 1)
    def _():
        greet({"pair": here + 1})

    lane = lax.broadcasted_iota(jnp.int32, (LABEL_ROWS, LANES), 1)
    places = [order_ref[mu_ref[0, t]] for t in range(tiles)]
    target = jnp.full((LABEL_ROWS, LANES), -1, jnp.int32)
    slots = jnp.full((LABEL_ROWS, LANES), -1, jnp.int32)
    for t in range(tiles):
        rank = jnp.int32(0)
        for u in range(t):
            rank = rank + (places[u] // (ao_dev // width) == places[t] // (ao_dev // width)).astype(jnp.int32)
        mine = (lane >= t * width) & (lane < (t + 1) * width)
        within = lane - t * width
        target = jnp.where(mine, places[t] * width + within, target)
        slots = jnp.where(mine, (here * CAP + rank) * width + within, slots)
    meta[here, 0] = target
    meta[here, 1] = slots

    if padded > rows:
        for layer in range(npair):
            held[layer, rows:padded, :] = jnp.zeros((padded - rows, held.shape[2]), held.dtype)

    row_in_block = lax.broadcasted_iota(jnp.int32, (width, nocc), 0)
    packed = aux_rows // 2 * width
    low_half = lax.broadcasted_iota(jnp.int32, (packed, 2 * nocc), 1) < nocc
    row_in_tile = lax.broadcasted_iota(jnp.int32, (packed, 2 * nocc), 0) % width

    def transform(t):
        parts = []
        for l in range(partners):
            block = lam_ref[t, l]
            parts.append(jnp.where(row_in_block < size_ref[block], coeffs_ref[block], 0.0))
        picked = jnp.concatenate(parts, axis=0)
        picked = jnp.concatenate([picked, picked], axis=1)
        full = jnp.dot(
            integrals_ref[t].reshape(aux_rows * width, depth), picked,
            precision=lax.Precision.HIGHEST, preferred_element_type=jnp.float32,
        )
        half = jnp.where(low_half, full[:packed], full[packed:])
        half = jnp.where(row_in_tile < size_ref[mu_ref[0, t]], half, 0.0).astype(held.dtype)
        for j in range(aux_rows // 2):
            held[here, t * width:(t + 1) * width, j * 2 * nocc:(j + 1) * 2 * nocc] = half[j * width:(j + 1) * width]

    def move(layer, part, step):
        sem = (out_left if step < 0 else out_right).at[layer, part]
        piece = held.at[layer, pl.ds(part * chunk, chunk)]
        return pltpu.make_async_remote_copy(
            src_ref=piece, dst_ref=piece, send_sem=sem, recv_sem=in_sem.at[layer, part],
            device_id={"pair": here + step}, device_id_type=MESH,
        )

    def move_meta(layer, step):
        sem = (meta_left if step < 0 else meta_right).at[layer]
        return pltpu.make_async_remote_copy(
            src_ref=meta.at[layer], dst_ref=meta.at[layer], send_sem=sem, recv_sem=meta_in.at[layer],
            device_id={"pair": here + step}, device_id_type=MESH,
        )

    def push(layer, part, step):
        move(layer, part, step).start()
        if part == 1:
            move_meta(layer, step).start()

    def take(layer, part, step):
        move(layer, part, step).wait_recv()
        if part == 1:
            move_meta(layer, step).wait_recv()

    for part in range(2):
        for t in range(part * tiles // 2, (part + 1) * tiles // 2):
            transform(t)
        if part == 0:
            before = (here + npair - 1) // npair
            after = (2 * npair - 2 - here) // npair
            pl.semaphore_wait(barrier, naux - 1 + before + after)

        @pl.when(here < npair - 1)
        def _():
            push(here, part, 1)

        @pl.when(here > 0)
        def _():
            push(here, part, -1)

    for hops in range(1, npair):
        for part in range(2):

            @pl.when(here >= hops)
            def _():
                take(here - hops, part, -1)

                @pl.when(here < npair - 1)
                def _():
                    push(here - hops, part, 1)

            @pl.when(here + hops < npair)
            def _():
                take(here + hops, part, 1)

                @pl.when(here > 0)
                def _():
                    push(here + hops, part, -1)

    stacked = held[...].reshape(npair * padded, held.shape[2])
    targets = jnp.concatenate([meta[k, 0, 0:1, :] for k in range(npair)], axis=1)
    slotted = jnp.concatenate([meta[k, 1, 0:1, :] for k in range(npair)], axis=1)
    first = here * ao_dev
    slotted = jnp.where((targets >= first) & (targets < first + ao_dev), slotted, -1)
    select = (
        lax.broadcasted_iota(jnp.int32, (slot_rows, npair * padded), 0) == slotted
    ).astype(jnp.float32).astype(jnp.bfloat16)
    local = jnp.broadcast_to((targets - first + 1).astype(jnp.float32), (16, npair * padded)).astype(jnp.bfloat16)
    local = jnp.where(slotted >= 0, local.astype(jnp.float32), 0.0).astype(jnp.bfloat16)
    labels = lax.dot_general(local, select, (((1,), (1,)), ((), ())), preferred_element_type=jnp.float32)
    labels = labels[:LABEL_ROWS]
    owned = jnp.dot(select, stacked, preferred_element_type=jnp.float32).astype(jnp.bfloat16)
    wanted = lax.broadcasted_iota(jnp.int32, (cols, npair * padded), 0)

    def partial_sum(dest):
        spread = (wanted + dest * cols == targets).astype(jnp.float32).astype(jnp.bfloat16)
        fitted = jnp.dot(spread, stacked, preferred_element_type=jnp.float32).astype(jnp.bfloat16)
        return lax.dot_general(owned, fitted, (((1,), (1,)), ((), ())), preferred_element_type=jnp.float32)

    def ship(offset):
        return pltpu.make_async_remote_copy(
            src_ref=sent.at[offset], dst_ref=arrived.at[offset],
            send_sem=sum_out.at[offset], recv_sem=sum_in.at[offset],
            device_id={"aux": mirrored(column, offset)}, device_id_type=MESH,
        )

    out_row = (lax.broadcasted_iota(jnp.int32, (ao_dev, slot_rows), 0) + 1).astype(jnp.float32)

    def place(label, value):
        spread = (out_row == label).astype(jnp.float32).astype(jnp.bfloat16)
        high = value.astype(jnp.bfloat16)
        low = (value - high.astype(jnp.float32)).astype(jnp.bfloat16)
        return jnp.dot(
            jnp.concatenate([spread, spread], axis=1), jnp.concatenate([high, low], axis=0),
            preferred_element_type=jnp.float32,
        )

    for offset in range(naux - 1, 0, -1):
        sent[offset, :slot_rows] = partial_sum(mirrored(column, offset))
        sent[offset, slot_rows:] = labels
        ship(offset).start()
    total = place(labels[0:1], partial_sum(column))
    for offset in range(1, naux):
        ship(offset).wait_recv()
        total = total + place(arrived[offset, slot_rows:slot_rows + 1], arrived[offset, :slot_rows])
    out_ref[...] = total

    for offset in range(1, naux):
        ship(offset).wait_send()
    for layer in range(npair):
        for part in range(2):

            @pl.when((here < npair - 1) & (here >= layer))
            def _():
                move(layer, part, 1).wait_send()
                if part == 1:
                    move_meta(layer, 1).wait_send()

            @pl.when((here > 0) & (here <= layer))
            def _():
                move(layer, part, -1).wait_send()
                if part == 1:
                    move_meta(layer, -1).wait_send()


def fused(integrals, mu_list, lam_list, coeffs, block_size, block_order):
    tiles, aux_rows, width, _ = integrals.shape
    nblk, _, nocc = coeffs.shape
    npair = lax.axis_size("pair")
    naux = lax.axis_size("aux")
    ao_dev = nblk // npair * width
    cols = nblk * width // naux
    summed_rows = npair * CAP * width + LABEL_ROWS
    vmem = pl.BlockSpec(memory_space=pltpu.VMEM)
    smem = pl.BlockSpec(memory_space=pltpu.SMEM)
    dma = pltpu.SemaphoreType.DMA
    return pl.pallas_call(
        functools.partial(exchange_kernel, npair, naux),
        out_shape=jax.ShapeDtypeStruct((ao_dev, cols), jnp.float32),
        in_specs=[smem, smem, smem, smem, vmem, vmem],
        out_specs=vmem,
        scratch_shapes=[
            pltpu.VMEM((npair, LANES, aux_rows * nocc), jnp.bfloat16),
            pltpu.VMEM((npair, 2, LABEL_ROWS, LANES), jnp.int32),
            pltpu.VMEM((naux, summed_rows, cols), jnp.float32),
            pltpu.VMEM((naux, summed_rows, cols), jnp.float32),
            dma((npair, 2)), dma((npair, 2)), dma((npair, 2)),
            dma((npair,)), dma((npair,)), dma((npair,)),
            dma((naux,)), dma((naux,)),
        ],
        compiler_params=pltpu.CompilerParams(
            collective_id=0, has_side_effects=True, vmem_limit_bytes=48 * 1024 * 1024
        ),
    )(mu_list, lam_list[0], block_size, block_order, integrals, coeffs)


def fits(integrals, mu_list, lam_list, coeffs, block_size, block_order):
    tiles, aux_rows, width, depth = integrals.shape
    nblk, _, nocc = coeffs.shape
    npair = lax.axis_size("pair")
    naux = lax.axis_size("aux")
    return (
        tiles % 2 == 0
        and tiles * width <= LANES
        and npair * CAP * width == LANES
        and nblk * width // naux == LANES
        and 2 * nocc == LANES
        and aux_rows % 2 == 0
        and width % 16 == 0
        and nblk // npair * width <= 256
        and naux & (naux - 1) == 0
    )


def device(*arrays):
    return fused(*arrays) if fits(*arrays) else body(*arrays)


def solution(mesh):
    return jax.shard_map(
        device,
        mesh=mesh,
        in_specs=(
            P("pair", "aux", None, None),
            P("aux", "pair"),
            P("aux", "pair", None),
            P(),
            P(),
            P(),
        ),
        out_specs=P("pair", "aux"),
        check_vma=False,
    )
```

```python
import functools

import jax
import jax.numpy as jnp
from jax import lax
from jax.experimental import pallas as pl
from jax.experimental.pallas import tpu as pltpu
from jax.sharding import PartitionSpec as P

CAP = 2
LANES = 128
LABEL_ROWS = 8
MESH = pl.DeviceIdType.MESH


def crossed(left, right):
    return lax.dot_general(
        left, right, (((1,), (1,)), ((), ())), preferred_element_type=jnp.float32
    )


def body(integrals, mu_list, lam_list, coeffs, block_size, block_order):
    tiles = integrals.shape[0]
    aux_rows = integrals.shape[1]
    width = integrals.shape[2]
    nblk, _, nocc = coeffs.shape
    npair = lax.axis_size("pair")
    here = lax.axis_index("pair")
    blk_dev = nblk // npair
    ao_dev = blk_dev * width
    slot_count = npair * CAP
    span = jnp.arange(width, dtype=jnp.int32)
    live = (span[None, :] < block_size[:, None]).astype(jnp.float32)
    masked = coeffs * live[:, :, None]
    picked = masked[lam_list[0]].reshape(tiles, -1, nocc)
    half = jnp.einsum("tqmk,tki->tmqi", integrals, picked, precision=lax.Precision.HIGHEST)
    half = half.astype(jnp.bfloat16).reshape(tiles, width * aux_rows * nocc)
    place = block_order[mu_list[0]]
    owner = place // blk_dev
    local = place % blk_dev
    order_ids = jnp.arange(tiles, dtype=jnp.int32)
    earlier = (owner[None, :] == owner[:, None]) & (order_ids[None, :] < order_ids[:, None])
    rank = jnp.sum(earlier.astype(jnp.int32), axis=1)
    slot = owner * CAP + rank
    select = jnp.arange(slot_count, dtype=jnp.int32)[:, None] == slot[None, :]
    outgoing = jnp.dot(
        select.astype(jnp.bfloat16), half, preferred_element_type=jnp.float32
    ).astype(jnp.bfloat16)
    outgoing = outgoing.reshape(npair, CAP, width * aux_rows * nocc)
    labels = jnp.sum(jnp.where(select, local[None, :] + 1, 0), axis=1) - 1
    labels = labels.reshape(npair, CAP)
    incoming, labels_in = (
        lax.all_to_all(outgoing, "pair", split_axis=0, concat_axis=0, tiled=True),
        lax.all_to_all(labels, "pair", split_axis=0, concat_axis=0, tiled=True),
    )
    assign = (
        labels_in.reshape(-1)[None, :] == jnp.arange(blk_dev, dtype=jnp.int32)[:, None]
    ).astype(jnp.bfloat16)
    fitted = jnp.dot(assign, incoming.reshape(slot_count, -1), preferred_element_type=jnp.float32)
    fitted = fitted.astype(jnp.bfloat16).reshape(ao_dev, aux_rows * nocc)
    partial_value = crossed(fitted, lax.all_gather(fitted, "pair", axis=0, tiled=True))
    summed = lax.psum_scatter(partial_value, "aux", scatter_dimension=1, tiled=True)
    posmat = (block_order[None, :] == jnp.arange(nblk, dtype=jnp.int32)[:, None]).astype(
        jnp.float32
    )
    live_pos = jnp.dot(posmat, live, precision=lax.Precision.HIGHEST).reshape(-1)
    cols = summed.shape[1]
    row_mask = lax.dynamic_slice_in_dim(live_pos, here * ao_dev, ao_dev, 0)
    col_mask = lax.dynamic_slice_in_dim(live_pos, lax.axis_index("aux") * cols, cols, 0)
    return summed * row_mask[:, None] * col_mask[None, :]


def mirrored(index, offset):
    result = index
    bit = 1
    while bit <= offset:
        if offset & bit:
            result = result + bit * (1 - 2 * ((index // bit) % 2))
        bit *= 2
    return result


def exchange_kernel(
    npair, naux, parts, mu_ref, lam_ref, size_ref, order_ref, integrals_hbm, coeffs_hbm, out_ref,
    integrals_ref, coeffs_ref, load_sem, held, meta, sent, arrived, out_left, out_right, in_sem, meta_left, meta_right, meta_in, sum_out, sum_in,
):
    tiles, aux_rows, width, depth = integrals_ref.shape
    nocc = coeffs_ref.shape[2]
    partners = depth // width
    ao_dev, cols = out_ref.shape
    rows = tiles * width
    padded = held.shape[1]
    chunk = rows // parts
    group = tiles // parts
    slot_rows = npair * CAP * width
    here = lax.axis_index("pair")
    column = lax.axis_index("aux")

    coeffs_load = pltpu.make_async_copy(coeffs_hbm, coeffs_ref, load_sem.at[parts])
    coeffs_load.start()
    loads = []
    for part in range(parts):
        wanted = pl.ds(part * group, group)
        loads.append(pltpu.make_async_copy(integrals_hbm.at[wanted], integrals_ref.at[wanted], load_sem.at[part]))
        loads[part].start()

    barrier = pltpu.get_barrier_semaphore()

    def greet(device):
        pl.semaphore_signal(barrier, inc=1, device_id=device, device_id_type=MESH)

    for offset in range(1, naux):
        greet({"aux": mirrored(column, offset)})

    @pl.when(here > 0)
    def _():
        greet({"pair": here - 1})

    @pl.when(here < npair - 1)
    def _():
        greet({"pair": here + 1})

    lane = lax.broadcasted_iota(jnp.int32, (LABEL_ROWS, LANES), 1)
    places = [order_ref[mu_ref[0, t]] for t in range(tiles)]
    target = jnp.full((LABEL_ROWS, LANES), -1, jnp.int32)
    slots = jnp.full((LABEL_ROWS, LANES), -1, jnp.int32)
    for t in range(tiles):
        rank = jnp.int32(0)
        for u in range(t):
            rank = rank + (places[u] // (ao_dev // width) == places[t] // (ao_dev // width)).astype(jnp.int32)
        mine = (lane >= t * width) & (lane < (t + 1) * width)
        within = lane - t * width
        target = jnp.where(mine, places[t] * width + within, target)
        slots = jnp.where(mine, (here * CAP + rank) * width + within, slots)
    meta[here, 0] = target
    meta[here, 1] = slots

    if padded > rows:
        for layer in range(npair):
            held[layer, rows:padded, :] = jnp.zeros((padded - rows, held.shape[2]), held.dtype)

    row_in_block = lax.broadcasted_iota(jnp.int32, (width, nocc), 0)
    packed = aux_rows // 2 * width
    low_half = lax.broadcasted_iota(jnp.int32, (packed, 2 * nocc), 1) < nocc
    row_in_tile = lax.broadcasted_iota(jnp.int32, (packed, 2 * nocc), 0) % width

    def transform(t):
        blocks = []
        for l in range(partners):
            block = lam_ref[t, 0, l]
            blocks.append(jnp.where(row_in_block < size_ref[block], coeffs_ref[block], 0.0))
        picked = jnp.concatenate(blocks, axis=0)
        picked = jnp.concatenate([picked, picked], axis=1)
        full = jnp.dot(
            integrals_ref[t].reshape(aux_rows * width, depth), picked,
            precision=lax.Precision.HIGHEST, preferred_element_type=jnp.float32,
        )
        half = jnp.where(low_half, full[:packed], full[packed:])
        half = jnp.where(row_in_tile < size_ref[mu_ref[0, t]], half, 0.0).astype(held.dtype)
        for j in range(aux_rows // 2):
            held[here, t * width:(t + 1) * width, j * 2 * nocc:(j + 1) * 2 * nocc] = half[j * width:(j + 1) * width]

    def move(layer, part, step):
        sem = (out_left if step < 0 else out_right).at[layer, part]
        piece = held.at[layer, pl.ds(part * chunk, chunk)]
        return pltpu.make_async_remote_copy(
            src_ref=piece, dst_ref=piece, send_sem=sem, recv_sem=in_sem.at[layer, part],
            device_id={"pair": here + step}, device_id_type=MESH,
        )

    def move_meta(layer, step):
        sem = (meta_left if step < 0 else meta_right).at[layer]
        return pltpu.make_async_remote_copy(
            src_ref=meta.at[layer], dst_ref=meta.at[layer], send_sem=sem, recv_sem=meta_in.at[layer],
            device_id={"pair": here + step}, device_id_type=MESH,
        )

    def push(layer, part, step):
        move(layer, part, step).start()
        if part == parts - 1:
            move_meta(layer, step).start()

    def take(layer, part, step):
        move(layer, part, step).wait_recv()
        if part == parts - 1:
            move_meta(layer, step).wait_recv()

    coeffs_load.wait()
    for part in range(parts):
        loads[part].wait()
        for t in range(part * group, (part + 1) * group):
            transform(t)
        if part == 0:
            before = (here + npair - 1) // npair
            after = (2 * npair - 2 - here) // npair
            pl.semaphore_wait(barrier, naux - 1 + before + after)

        @pl.when(here < npair - 1)
        def _():
            push(here, part, 1)

        @pl.when(here > 0)
        def _():
            push(here, part, -1)

    for hops in range(1, npair):
        for part in range(parts):

            @pl.when(here >= hops)
            def _():
                take(here - hops, part, -1)

                @pl.when(here < npair - 1)
                def _():
                    push(here - hops, part, 1)

            @pl.when(here + hops < npair)
            def _():
                take(here + hops, part, 1)

                @pl.when(here > 0)
                def _():
                    push(here + hops, part, -1)

    stacked = held[...].reshape(npair * padded, held.shape[2])
    targets = jnp.concatenate([meta[k, 0, 0:1, :] for k in range(npair)], axis=1)
    slotted = jnp.concatenate([meta[k, 1, 0:1, :] for k in range(npair)], axis=1)
    first = here * ao_dev
    slotted = jnp.where((targets >= first) & (targets < first + ao_dev), slotted, -1)
    select = (
        lax.broadcasted_iota(jnp.int32, (slot_rows, npair * padded), 0) == slotted
    ).astype(jnp.float32).astype(jnp.bfloat16)
    local = jnp.broadcast_to((targets - first + 1).astype(jnp.float32), (16, npair * padded)).astype(jnp.bfloat16)
    local = jnp.where(slotted >= 0, local.astype(jnp.float32), 0.0).astype(jnp.bfloat16)
    labels = lax.dot_general(local, select, (((1,), (1,)), ((), ())), preferred_element_type=jnp.float32)
    labels = labels[:LABEL_ROWS]
    owned = jnp.dot(select, stacked, preferred_element_type=jnp.float32).astype(jnp.bfloat16)
    wanted = lax.broadcasted_iota(jnp.int32, (cols, npair * padded), 0)

    def partial_sum(dest):
        spread = (wanted + dest * cols == targets).astype(jnp.float32).astype(jnp.bfloat16)
        fitted = jnp.dot(spread, stacked, preferred_element_type=jnp.float32).astype(jnp.bfloat16)
        return lax.dot_general(owned, fitted, (((1,), (1,)), ((), ())), preferred_element_type=jnp.float32)

    def ship(offset):
        return pltpu.make_async_remote_copy(
            src_ref=sent.at[offset], dst_ref=arrived.at[offset],
            send_sem=sum_out.at[offset], recv_sem=sum_in.at[offset],
            device_id={"aux": mirrored(column, offset)}, device_id_type=MESH,
        )

    out_row = (lax.broadcasted_iota(jnp.int32, (ao_dev, slot_rows), 0) + 1).astype(jnp.float32)

    def place(label, value):
        spread = (out_row == label).astype(jnp.float32).astype(jnp.bfloat16)
        high = value.astype(jnp.bfloat16)
        low = (value - high.astype(jnp.float32)).astype(jnp.bfloat16)
        return jnp.dot(
            jnp.concatenate([spread, spread], axis=1), jnp.concatenate([high, low], axis=0),
            preferred_element_type=jnp.float32,
        )

    for offset in range(naux - 1, 0, -1):
        sent[offset, :slot_rows] = partial_sum(mirrored(column, offset))
        sent[offset, slot_rows:] = labels
        ship(offset).start()
    total = place(labels[0:1], partial_sum(column))
    for offset in range(1, naux):
        ship(offset).wait_recv()
        total = total + place(arrived[offset, slot_rows:slot_rows + 1], arrived[offset, :slot_rows])
    out_ref[...] = total

    for offset in range(1, naux):
        ship(offset).wait_send()
    for layer in range(npair):
        for part in range(parts):

            @pl.when((here < npair - 1) & (here >= layer))
            def _():
                move(layer, part, 1).wait_send()
                if part == parts - 1:
                    move_meta(layer, 1).wait_send()

            @pl.when((here > 0) & (here <= layer))
            def _():
                move(layer, part, -1).wait_send()
                if part == parts - 1:
                    move_meta(layer, -1).wait_send()


def fused(integrals, mu_list, lam_list, coeffs, block_size, block_order):
    tiles, aux_rows, width, _ = integrals.shape
    nblk, _, nocc = coeffs.shape
    npair = lax.axis_size("pair")
    naux = lax.axis_size("aux")
    ao_dev = nblk // npair * width
    cols = nblk * width // naux
    summed_rows = npair * CAP * width + LABEL_ROWS
    vmem = pl.BlockSpec(memory_space=pltpu.VMEM)
    smem = pl.BlockSpec(memory_space=pltpu.SMEM)
    dma = pltpu.SemaphoreType.DMA
    anywhere = pl.BlockSpec(memory_space=pl.ANY)
    parts = 3 if tiles % 3 == 0 else 1
    return pl.pallas_call(
        functools.partial(exchange_kernel, npair, naux, parts),
        out_shape=jax.ShapeDtypeStruct((ao_dev, cols), jnp.float32),
        in_specs=[smem, smem, smem, smem, anywhere, anywhere],
        out_specs=vmem,
        scratch_shapes=[
            pltpu.VMEM(integrals.shape, jnp.float32),
            pltpu.VMEM(coeffs.shape, jnp.float32),
            dma((parts + 1,)),
            pltpu.VMEM((npair, LANES, aux_rows * nocc), jnp.bfloat16),
            pltpu.VMEM((npair, 2, LABEL_ROWS, LANES), jnp.int32),
            pltpu.VMEM((naux, summed_rows, cols), jnp.float32),
            pltpu.VMEM((naux, summed_rows, cols), jnp.float32),
            dma((npair, parts)), dma((npair, parts)), dma((npair, parts)),
            dma((npair,)), dma((npair,)), dma((npair,)),
            dma((naux,)), dma((naux,)),
        ],
        compiler_params=pltpu.CompilerParams(
            collective_id=0, has_side_effects=True, vmem_limit_bytes=60 * 1024 * 1024
        ),
    )(mu_list, jnp.transpose(lam_list, (1, 0, 2)), block_size, block_order, integrals, coeffs)


def fits(integrals, mu_list, lam_list, coeffs, block_size, block_order):
    tiles, aux_rows, width, depth = integrals.shape
    nblk, _, nocc = coeffs.shape
    npair = lax.axis_size("pair")
    naux = lax.axis_size("aux")
    return (
        tiles * width <= LANES
        and npair * CAP * width == LANES
        and nblk * width // naux == LANES
        and 2 * nocc == LANES
        and aux_rows % 2 == 0
        and width % 16 == 0
        and nblk // npair * width <= 256
        and naux & (naux - 1) == 0
    )


def device(*arrays):
    return fused(*arrays) if fits(*arrays) else body(*arrays)


def solution(mesh):
    return jax.shard_map(
        device,
        mesh=mesh,
        in_specs=(
            P("pair", "aux", None, None),
            P("aux", "pair"),
            P("aux", "pair", None),
            P(),
            P(),
            P(),
        ),
        out_specs=P("pair", "aux"),
        check_vma=False,
    )
```

```python
import functools

import jax
import jax.numpy as jnp
from jax import lax
from jax.experimental import pallas as pl
from jax.experimental.pallas import tpu as pltpu
from jax.sharding import PartitionSpec as P

CAP = 2
LANES = 128
LABEL_ROWS = 8
MESH = pl.DeviceIdType.MESH


def crossed(left, right):
    return lax.dot_general(
        left, right, (((1,), (1,)), ((), ())), preferred_element_type=jnp.float32
    )


def body(integrals, mu_list, lam_list, coeffs, block_size, block_order):
    tiles = integrals.shape[0]
    aux_rows = integrals.shape[1]
    width = integrals.shape[2]
    nblk, _, nocc = coeffs.shape
    npair = lax.axis_size("pair")
    here = lax.axis_index("pair")
    blk_dev = nblk // npair
    ao_dev = blk_dev * width
    slot_count = npair * CAP
    span = jnp.arange(width, dtype=jnp.int32)
    live = (span[None, :] < block_size[:, None]).astype(jnp.float32)
    masked = coeffs * live[:, :, None]
    picked = masked[lam_list[0]].reshape(tiles, -1, nocc)
    half = jnp.einsum("tqmk,tki->tmqi", integrals, picked, precision=lax.Precision.HIGHEST)
    half = half.astype(jnp.bfloat16).reshape(tiles, width * aux_rows * nocc)
    place = block_order[mu_list[0]]
    owner = place // blk_dev
    local = place % blk_dev
    order_ids = jnp.arange(tiles, dtype=jnp.int32)
    earlier = (owner[None, :] == owner[:, None]) & (order_ids[None, :] < order_ids[:, None])
    rank = jnp.sum(earlier.astype(jnp.int32), axis=1)
    slot = owner * CAP + rank
    select = jnp.arange(slot_count, dtype=jnp.int32)[:, None] == slot[None, :]
    outgoing = jnp.dot(
        select.astype(jnp.bfloat16), half, preferred_element_type=jnp.float32
    ).astype(jnp.bfloat16)
    outgoing = outgoing.reshape(npair, CAP, width * aux_rows * nocc)
    labels = jnp.sum(jnp.where(select, local[None, :] + 1, 0), axis=1) - 1
    labels = labels.reshape(npair, CAP)
    incoming, labels_in = (
        lax.all_to_all(outgoing, "pair", split_axis=0, concat_axis=0, tiled=True),
        lax.all_to_all(labels, "pair", split_axis=0, concat_axis=0, tiled=True),
    )
    assign = (
        labels_in.reshape(-1)[None, :] == jnp.arange(blk_dev, dtype=jnp.int32)[:, None]
    ).astype(jnp.bfloat16)
    fitted = jnp.dot(assign, incoming.reshape(slot_count, -1), preferred_element_type=jnp.float32)
    fitted = fitted.astype(jnp.bfloat16).reshape(ao_dev, aux_rows * nocc)
    partial_value = crossed(fitted, lax.all_gather(fitted, "pair", axis=0, tiled=True))
    summed = lax.psum_scatter(partial_value, "aux", scatter_dimension=1, tiled=True)
    posmat = (block_order[None, :] == jnp.arange(nblk, dtype=jnp.int32)[:, None]).astype(
        jnp.float32
    )
    live_pos = jnp.dot(posmat, live, precision=lax.Precision.HIGHEST).reshape(-1)
    cols = summed.shape[1]
    row_mask = lax.dynamic_slice_in_dim(live_pos, here * ao_dev, ao_dev, 0)
    col_mask = lax.dynamic_slice_in_dim(live_pos, lax.axis_index("aux") * cols, cols, 0)
    return summed * row_mask[:, None] * col_mask[None, :]


def mirrored(index, offset):
    result = index
    bit = 1
    while bit <= offset:
        if offset & bit:
            result = result + bit * (1 - 2 * ((index // bit) % 2))
        bit *= 2
    return result


def exchange_kernel(
    npair, naux, parts, mu_hbm, lam_hbm, size_hbm, order_hbm, integrals_hbm, coeffs_hbm, out_ref,
    mu_ref, lam_ref, size_ref, order_ref, scalar_sem, integrals_ref, coeffs_ref, load_sem, held, meta, sent, arrived, out_left, out_right, in_sem, meta_left, meta_right, meta_in, sum_out, sum_in,
):
    tiles, aux_rows, width, depth = integrals_ref.shape
    nocc = coeffs_ref.shape[2]
    partners = depth // width
    ao_dev, cols = out_ref.shape
    rows = tiles * width
    padded = held.shape[1]
    chunk = rows // parts
    group = tiles // parts
    slot_rows = npair * CAP * width
    here = lax.axis_index("pair")
    column = lax.axis_index("aux")
    low_layer = here < npair // 2
    high_layer = here >= npair // 2

    scalar_loads = []
    for source, dest in ((mu_hbm, mu_ref), (lam_hbm, lam_ref), (size_hbm, size_ref), (order_hbm, order_ref)):
        scalar_loads.append(pltpu.make_async_copy(source, dest, scalar_sem.at[len(scalar_loads)]))
        scalar_loads[-1].start()
    coeffs_load = pltpu.make_async_copy(coeffs_hbm, coeffs_ref, load_sem.at[parts])
    coeffs_load.start()
    loads = []
    for part in range(parts):
        wanted = pl.ds(part * group, group)
        loads.append(pltpu.make_async_copy(integrals_hbm.at[wanted], integrals_ref.at[wanted], load_sem.at[part]))
        loads[part].start()

    barrier = pltpu.get_barrier_semaphore()

    def greet(device):
        pl.semaphore_signal(barrier, inc=1, device_id=device, device_id_type=MESH)

    for offset in range(1, naux):
        greet({"aux": mirrored(column, offset)})

    @pl.when(here > 0)
    def _():
        greet({"pair": here - 1})

    @pl.when(here < npair - 1)
    def _():
        greet({"pair": here + 1})

    for load in scalar_loads:
        load.wait()
    lane = lax.broadcasted_iota(jnp.int32, (LABEL_ROWS, LANES), 1)
    places = [order_ref[mu_ref[0, t]] for t in range(tiles)]
    target = jnp.full((LABEL_ROWS, LANES), -1, jnp.int32)
    slots = jnp.full((LABEL_ROWS, LANES), -1, jnp.int32)
    for t in range(tiles):
        rank = jnp.int32(0)
        for u in range(t):
            rank = rank + (places[u] // (ao_dev // width) == places[t] // (ao_dev // width)).astype(jnp.int32)
        mine = (lane >= t * width) & (lane < (t + 1) * width)
        within = lane - t * width
        target = jnp.where(mine, places[t] * width + within, target)
        slots = jnp.where(mine, (here * CAP + rank) * width + within, slots)
    meta[here, 0] = target
    meta[here, 1] = slots

    if padded > rows:
        for layer in range(npair):
            held[layer, rows:padded, :] = jnp.zeros((padded - rows, held.shape[2]), held.dtype)

    row_in_block = lax.broadcasted_iota(jnp.int32, (width, nocc), 0)
    packed = aux_rows // 2 * width
    low_half = lax.broadcasted_iota(jnp.int32, (packed, 2 * nocc), 1) < nocc
    row_in_tile = lax.broadcasted_iota(jnp.int32, (packed, 2 * nocc), 0) % width

    def transform(t):
        blocks = []
        for l in range(partners):
            block = lam_ref[t, 0, l]
            blocks.append(jnp.where(row_in_block < size_ref[block], coeffs_ref[block], 0.0))
        picked = jnp.concatenate(blocks, axis=0)
        picked = jnp.concatenate([picked, picked], axis=1)
        full = jnp.dot(
            integrals_ref[t].reshape(aux_rows * width, depth), picked,
            precision=lax.Precision.HIGHEST, preferred_element_type=jnp.float32,
        )
        half = jnp.where(low_half, full[:packed], full[packed:])
        half = jnp.where(row_in_tile < size_ref[mu_ref[0, t]], half, 0.0).astype(held.dtype)
        for j in range(aux_rows // 2):
            held[here, t * width:(t + 1) * width, j * 2 * nocc:(j + 1) * 2 * nocc] = half[j * width:(j + 1) * width]

    def move(layer, part, step):
        sem = (out_left if step < 0 else out_right).at[layer, part]
        piece = held.at[layer, pl.ds(part * chunk, chunk)]
        return pltpu.make_async_remote_copy(
            src_ref=piece, dst_ref=piece, send_sem=sem, recv_sem=in_sem.at[layer, part],
            device_id={"pair": here + step}, device_id_type=MESH,
        )

    def move_meta(layer, step):
        sem = (meta_left if step < 0 else meta_right).at[layer]
        return pltpu.make_async_remote_copy(
            src_ref=meta.at[layer], dst_ref=meta.at[layer], send_sem=sem, recv_sem=meta_in.at[layer],
            device_id={"pair": here + step}, device_id_type=MESH,
        )

    def push(layer, part, step):
        move(layer, part, step).start()
        if part == parts - 1:
            move_meta(layer, step).start()

    def take(layer, part, step):
        move(layer, part, step).wait_recv()
        if part == parts - 1:
            move_meta(layer, step).wait_recv()

    coeffs_load.wait()
    for part in range(parts):
        loads[part].wait()
        for t in range(part * group, (part + 1) * group):
            transform(t)
        if part == 0:
            before = (here + npair - 1) // npair
            after = (2 * npair - 2 - here) // npair
            pl.semaphore_wait(barrier, naux - 1 + before + after)

        @pl.when((here > 0) & low_layer)
        def _():
            push(here, part, -1)

        @pl.when(here < npair - 1)
        def _():
            push(here, part, 1)

        @pl.when((here > 0) & high_layer)
        def _():
            push(here, part, -1)

    def pass_on(hops, part, step):
        take(here + step * hops, part, step)
        onward = here > 0 if step > 0 else here < npair - 1

        @pl.when(onward)
        def _():
            push(here + step * hops, part, step * -1)

    for hops in range(1, npair):
        for part in range(parts):

            @pl.when((here + hops < npair) & low_layer)
            def _():
                pass_on(hops, part, 1)

            @pl.when(here >= hops)
            def _():
                pass_on(hops, part, -1)

            @pl.when((here + hops < npair) & high_layer)
            def _():
                pass_on(hops, part, 1)

    stacked = held[...].reshape(npair * padded, held.shape[2])
    targets = jnp.concatenate([meta[k, 0, 0:1, :] for k in range(npair)], axis=1)
    slotted = jnp.concatenate([meta[k, 1, 0:1, :] for k in range(npair)], axis=1)
    first = here * ao_dev
    slotted = jnp.where((targets >= first) & (targets < first + ao_dev), slotted, -1)
    select = (
        lax.broadcasted_iota(jnp.int32, (slot_rows, npair * padded), 0) == slotted
    ).astype(jnp.float32).astype(jnp.bfloat16)
    local = jnp.broadcast_to((targets - first + 1).astype(jnp.float32), (16, npair * padded)).astype(jnp.bfloat16)
    local = jnp.where(slotted >= 0, local.astype(jnp.float32), 0.0).astype(jnp.bfloat16)
    labels = lax.dot_general(local, select, (((1,), (1,)), ((), ())), preferred_element_type=jnp.float32)
    labels = labels[:LABEL_ROWS]
    owned = jnp.dot(select, stacked, preferred_element_type=jnp.float32).astype(jnp.bfloat16)
    wanted = lax.broadcasted_iota(jnp.int32, (cols, npair * padded), 0)

    def partial_sum(dest):
        spread = (wanted + dest * cols == targets).astype(jnp.float32).astype(jnp.bfloat16)
        fitted = jnp.dot(spread, stacked, preferred_element_type=jnp.float32).astype(jnp.bfloat16)
        return lax.dot_general(owned, fitted, (((1,), (1,)), ((), ())), preferred_element_type=jnp.float32)

    def ship(offset):
        return pltpu.make_async_remote_copy(
            src_ref=sent.at[offset], dst_ref=arrived.at[offset],
            send_sem=sum_out.at[offset], recv_sem=sum_in.at[offset],
            device_id={"aux": mirrored(column, offset)}, device_id_type=MESH,
        )

    out_row = (lax.broadcasted_iota(jnp.int32, (ao_dev, slot_rows), 0) + 1).astype(jnp.float32)

    def place(label, value):
        spread = (out_row == label).astype(jnp.float32).astype(jnp.bfloat16)
        high = value.astype(jnp.bfloat16)
        low = (value - high.astype(jnp.float32)).astype(jnp.bfloat16)
        return jnp.dot(
            jnp.concatenate([spread, spread], axis=1), jnp.concatenate([high, low], axis=0),
            preferred_element_type=jnp.float32,
        )

    for offset in range(naux - 1, 0, -1):
        sent[offset, :slot_rows] = partial_sum(mirrored(column, offset))
        sent[offset, slot_rows:] = labels
        ship(offset).start()
    total = place(labels[0:1], partial_sum(column))
    for offset in range(1, naux):
        ship(offset).wait_recv()
        total = total + place(arrived[offset, slot_rows:slot_rows + 1], arrived[offset, :slot_rows])
    out_ref[...] = total

    for offset in range(1, naux):
        ship(offset).wait_send()
    for layer in range(npair):
        for part in range(parts):

            @pl.when((here < npair - 1) & (here >= layer))
            def _():
                move(layer, part, 1).wait_send()
                if part == parts - 1:
                    move_meta(layer, 1).wait_send()

            @pl.when((here > 0) & (here <= layer))
            def _():
                move(layer, part, -1).wait_send()
                if part == parts - 1:
                    move_meta(layer, -1).wait_send()


def fused(integrals, mu_list, lam_list, coeffs, block_size, block_order):
    tiles, aux_rows, width, _ = integrals.shape
    nblk, _, nocc = coeffs.shape
    npair = lax.axis_size("pair")
    naux = lax.axis_size("aux")
    ao_dev = nblk // npair * width
    cols = nblk * width // naux
    summed_rows = npair * CAP * width + LABEL_ROWS
    vmem = pl.BlockSpec(memory_space=pltpu.VMEM)
    dma = pltpu.SemaphoreType.DMA
    hbm = pl.BlockSpec(memory_space=pltpu.HBM)
    parts = 3 if tiles % 3 == 0 else 1
    return pl.pallas_call(
        functools.partial(exchange_kernel, npair, naux, parts),
        out_shape=jax.ShapeDtypeStruct((ao_dev, cols), jnp.float32),
        in_specs=[hbm] * 6,
        out_specs=vmem,
        scratch_shapes=[
            pltpu.SMEM(mu_list.shape, jnp.int32),
            pltpu.SMEM((tiles, 1, lam_list.shape[2]), jnp.int32),
            pltpu.SMEM(block_size.shape, jnp.int32),
            pltpu.SMEM(block_order.shape, jnp.int32),
            dma((4,)),
            pltpu.VMEM(integrals.shape, jnp.float32),
            pltpu.VMEM(coeffs.shape, jnp.float32),
            dma((parts + 1,)),
            pltpu.VMEM((npair, LANES, aux_rows * nocc), jnp.bfloat16),
            pltpu.VMEM((npair, 2, LABEL_ROWS, LANES), jnp.int32),
            pltpu.VMEM((naux, summed_rows, cols), jnp.float32),
            pltpu.VMEM((naux, summed_rows, cols), jnp.float32),
            dma((npair, parts)), dma((npair, parts)), dma((npair, parts)),
            dma((npair,)), dma((npair,)), dma((npair,)),
            dma((naux,)), dma((naux,)),
        ],
        compiler_params=pltpu.CompilerParams(
            collective_id=0, has_side_effects=True, vmem_limit_bytes=60 * 1024 * 1024
        ),
    )(mu_list, jnp.transpose(lam_list, (1, 0, 2)), block_size, block_order, integrals, coeffs)


def fits(integrals, mu_list, lam_list, coeffs, block_size, block_order):
    tiles, aux_rows, width, depth = integrals.shape
    nblk, _, nocc = coeffs.shape
    npair = lax.axis_size("pair")
    naux = lax.axis_size("aux")
    return (
        tiles * width <= LANES
        and npair * CAP * width == LANES
        and nblk * width // naux == LANES
        and 2 * nocc == LANES
        and aux_rows % 2 == 0
        and width % 16 == 0
        and nblk // npair * width <= 256
        and naux & (naux - 1) == 0
    )


def device(*arrays):
    return fused(*arrays) if fits(*arrays) else body(*arrays)


def solution(mesh):
    return jax.shard_map(
        device,
        mesh=mesh,
        in_specs=(
            P("pair", "aux", None, None),
            P("aux", "pair"),
            P("aux", "pair", None),
            P(),
            P(),
            P(),
        ),
        out_specs=P("pair", "aux"),
        check_vma=False,
    )
```

```python
import functools

import jax
import jax.numpy as jnp
from jax import lax
from jax.experimental import pallas as pl
from jax.experimental.pallas import tpu as pltpu
from jax.sharding import PartitionSpec as P

CAP = 2
LANES = 128
LABEL_ROWS = 8
MESH = pl.DeviceIdType.MESH


def crossed(left, right):
    return lax.dot_general(
        left, right, (((1,), (1,)), ((), ())), preferred_element_type=jnp.float32
    )


def body(integrals, mu_list, lam_list, coeffs, block_size, block_order):
    tiles = integrals.shape[0]
    aux_rows = integrals.shape[1]
    width = integrals.shape[2]
    nblk, _, nocc = coeffs.shape
    npair = lax.axis_size("pair")
    here = lax.axis_index("pair")
    blk_dev = nblk // npair
    ao_dev = blk_dev * width
    slot_count = npair * CAP
    span = jnp.arange(width, dtype=jnp.int32)
    live = (span[None, :] < block_size[:, None]).astype(jnp.float32)
    masked = coeffs * live[:, :, None]
    picked = masked[lam_list[0]].reshape(tiles, -1, nocc)
    half = jnp.einsum("tqmk,tki->tmqi", integrals, picked, precision=lax.Precision.HIGHEST)
    half = half.astype(jnp.bfloat16).reshape(tiles, width * aux_rows * nocc)
    place = block_order[mu_list[0]]
    owner = place // blk_dev
    local = place % blk_dev
    order_ids = jnp.arange(tiles, dtype=jnp.int32)
    earlier = (owner[None, :] == owner[:, None]) & (order_ids[None, :] < order_ids[:, None])
    rank = jnp.sum(earlier.astype(jnp.int32), axis=1)
    slot = owner * CAP + rank
    select = jnp.arange(slot_count, dtype=jnp.int32)[:, None] == slot[None, :]
    outgoing = jnp.dot(
        select.astype(jnp.bfloat16), half, preferred_element_type=jnp.float32
    ).astype(jnp.bfloat16)
    outgoing = outgoing.reshape(npair, CAP, width * aux_rows * nocc)
    labels = jnp.sum(jnp.where(select, local[None, :] + 1, 0), axis=1) - 1
    labels = labels.reshape(npair, CAP)
    incoming, labels_in = (
        lax.all_to_all(outgoing, "pair", split_axis=0, concat_axis=0, tiled=True),
        lax.all_to_all(labels, "pair", split_axis=0, concat_axis=0, tiled=True),
    )
    assign = (
        labels_in.reshape(-1)[None, :] == jnp.arange(blk_dev, dtype=jnp.int32)[:, None]
    ).astype(jnp.bfloat16)
    fitted = jnp.dot(assign, incoming.reshape(slot_count, -1), preferred_element_type=jnp.float32)
    fitted = fitted.astype(jnp.bfloat16).reshape(ao_dev, aux_rows * nocc)
    partial_value = crossed(fitted, lax.all_gather(fitted, "pair", axis=0, tiled=True))
    summed = lax.psum_scatter(partial_value, "aux", scatter_dimension=1, tiled=True)
    posmat = (block_order[None, :] == jnp.arange(nblk, dtype=jnp.int32)[:, None]).astype(
        jnp.float32
    )
    live_pos = jnp.dot(posmat, live, precision=lax.Precision.HIGHEST).reshape(-1)
    cols = summed.shape[1]
    row_mask = lax.dynamic_slice_in_dim(live_pos, here * ao_dev, ao_dev, 0)
    col_mask = lax.dynamic_slice_in_dim(live_pos, lax.axis_index("aux") * cols, cols, 0)
    return summed * row_mask[:, None] * col_mask[None, :]


def mirrored(index, offset):
    result = index
    bit = 1
    while bit <= offset:
        if offset & bit:
            result = result + bit * (1 - 2 * ((index // bit) % 2))
        bit *= 2
    return result


def exchange_kernel(
    npair, naux, parts, mu_hbm, lam_hbm, size_hbm, order_hbm, integrals_hbm, coeffs_hbm, out_ref,
    mu_ref, lam_ref, size_ref, order_ref, scalar_sem, integrals_ref, coeffs_ref, load_sem, held, meta, near_fitted, sent_near, near_in, sent_far, far_in, out_left, out_right, in_sem, meta_left, meta_right, meta_in,
    near_out, near_arrived, far_out, far_arrived,
):
    tiles, aux_rows, width, depth = integrals_ref.shape
    nocc = coeffs_ref.shape[2]
    partners = depth // width
    ao_dev, cols = out_ref.shape
    rows = tiles * width
    padded = held.shape[1]
    chunk = rows // parts
    group = tiles // parts
    here = lax.axis_index("pair")
    column = lax.axis_index("aux")
    low_layer = here < npair // 2
    high_layer = here >= npair // 2

    scalar_loads = []
    for source, dest in ((mu_hbm, mu_ref), (lam_hbm, lam_ref), (size_hbm, size_ref), (order_hbm, order_ref)):
        scalar_loads.append(pltpu.make_async_copy(source, dest, scalar_sem.at[len(scalar_loads)]))
        scalar_loads[-1].start()
    coeffs_load = pltpu.make_async_copy(coeffs_hbm, coeffs_ref, load_sem.at[parts])
    coeffs_load.start()
    loads = []
    for part in range(parts):
        wanted = pl.ds(part * group, group)
        loads.append(pltpu.make_async_copy(integrals_hbm.at[wanted], integrals_ref.at[wanted], load_sem.at[part]))
        loads[part].start()

    barrier = pltpu.get_barrier_semaphore()

    def greet(device):
        pl.semaphore_signal(barrier, inc=1, device_id=device, device_id_type=MESH)

    for offset in range(1, naux):
        greet({"aux": mirrored(column, offset)})

    @pl.when(here > 0)
    def _():
        greet({"pair": here - 1})

    @pl.when(here < npair - 1)
    def _():
        greet({"pair": here + 1})

    for load in scalar_loads:
        load.wait()
    lane = lax.broadcasted_iota(jnp.int32, (LABEL_ROWS, LANES), 1)
    places = [order_ref[mu_ref[0, t]] for t in range(tiles)]
    target = jnp.full((LABEL_ROWS, LANES), -1, jnp.int32)
    slots = jnp.full((LABEL_ROWS, LANES), -1, jnp.int32)
    for t in range(tiles):
        rank = jnp.int32(0)
        for u in range(t):
            rank = rank + (places[u] // (ao_dev // width) == places[t] // (ao_dev // width)).astype(jnp.int32)
        mine = (lane >= t * width) & (lane < (t + 1) * width)
        within = lane - t * width
        target = jnp.where(mine, places[t] * width + within, target)
        slots = jnp.where(mine, (here * CAP + rank) * width + within, slots)
    meta[here, 0] = target
    meta[here, 1] = slots

    if padded > rows:
        for layer in range(npair):
            held[layer, rows:padded, :] = jnp.zeros((padded - rows, held.shape[2]), held.dtype)

    row_in_block = lax.broadcasted_iota(jnp.int32, (width, nocc), 0)
    packed = aux_rows // 2 * width
    low_half = lax.broadcasted_iota(jnp.int32, (packed, 2 * nocc), 1) < nocc
    row_in_tile = lax.broadcasted_iota(jnp.int32, (packed, 2 * nocc), 0) % width

    def transform(t):
        blocks = []
        for l in range(partners):
            block = lam_ref[t, 0, l]
            blocks.append(jnp.where(row_in_block < size_ref[block], coeffs_ref[block], 0.0))
        picked = jnp.concatenate(blocks, axis=0)
        picked = jnp.concatenate([picked, picked], axis=1)
        full = jnp.dot(
            integrals_ref[t].reshape(aux_rows * width, depth), picked,
            precision=lax.Precision.HIGHEST, preferred_element_type=jnp.float32,
        )
        half = jnp.where(low_half, full[:packed], full[packed:])
        half = jnp.where(row_in_tile < size_ref[mu_ref[0, t]], half, 0.0).astype(held.dtype)
        for j in range(aux_rows // 2):
            held[here, t * width:(t + 1) * width, j * 2 * nocc:(j + 1) * 2 * nocc] = half[j * width:(j + 1) * width]

    def move(layer, part, step):
        sem = (out_left if step < 0 else out_right).at[layer, part]
        piece = held.at[layer, pl.ds(part * chunk, chunk)]
        return pltpu.make_async_remote_copy(
            src_ref=piece, dst_ref=piece, send_sem=sem, recv_sem=in_sem.at[layer, part],
            device_id={"pair": here + step}, device_id_type=MESH,
        )

    def move_meta(layer, step):
        sem = (meta_left if step < 0 else meta_right).at[layer]
        return pltpu.make_async_remote_copy(
            src_ref=meta.at[layer], dst_ref=meta.at[layer], send_sem=sem, recv_sem=meta_in.at[layer],
            device_id={"pair": here + step}, device_id_type=MESH,
        )

    def push(layer, part, step):
        move(layer, part, step).start()
        if part == parts - 1:
            move_meta(layer, step).start()

    def take(layer, part, step):
        move(layer, part, step).wait_recv()
        if part == parts - 1:
            move_meta(layer, step).wait_recv()

    coeffs_load.wait()
    for part in range(parts):
        loads[part].wait()
        for t in range(part * group, (part + 1) * group):
            transform(t)
        if part == 0:
            before = (here + npair - 1) // npair
            after = (2 * npair - 2 - here) // npair
            pl.semaphore_wait(barrier, naux - 1 + before + after)

        @pl.when((here > 0) & low_layer)
        def _():
            push(here, part, -1)

        @pl.when(here < npair - 1)
        def _():
            push(here, part, 1)

        @pl.when((here > 0) & high_layer)
        def _():
            push(here, part, -1)

    def pass_on(hops, part, step):
        take(here + step * hops, part, step)
        onward = here > 0 if step > 0 else here < npair - 1

        @pl.when(onward)
        def _():
            push(here + step * hops, part, step * -1)

    def gather_step(hops):
        for part in range(parts):

            @pl.when((here + hops < npair) & low_layer)
            def _():
                pass_on(hops, part, 1)

            @pl.when(here >= hops)
            def _():
                pass_on(hops, part, -1)

            @pl.when((here + hops < npair) & high_layer)
            def _():
                pass_on(hops, part, 1)

    def one_hot(rows_of, wanted_row):
        found = lax.broadcasted_iota(jnp.int32, (rows_of, wanted_row.shape[1]), 0) == wanted_row
        return found.astype(jnp.float32).astype(jnp.bfloat16)

    def times(left, right):
        return jnp.dot(left, right, preferred_element_type=jnp.float32)

    def label_row(local, select):
        local = jnp.broadcast_to(local.astype(jnp.float32), (16, local.shape[1])).astype(jnp.bfloat16)
        return crossed(local, select)[:LABEL_ROWS]

    def ship(source, dest, out_sems, in_sems, offset):
        return pltpu.make_async_remote_copy(
            src_ref=source.at[offset], dst_ref=dest.at[offset],
            send_sem=out_sems.at[offset], recv_sem=in_sems.at[offset],
            device_id={"aux": mirrored(column, offset)}, device_id_type=MESH,
        )

    def ship_near(offset):
        return ship(sent_near, near_in, near_out, near_arrived, offset)

    def ship_far(offset):
        return ship(sent_far, far_in, far_out, far_arrived, offset)

    for hops in range(1, npair - 1):
        gather_step(hops)

    upper = here // (npair // 2)
    far = (npair - 1) * (1 - upper)
    layers = npair - 1
    slots_of = CAP * width
    near_rows = layers * slots_of
    first = here * ao_dev

    near = held[pl.ds(upper, layers)].reshape(layers * padded, held.shape[2])
    near_targets = jnp.concatenate([meta[upper + k, 0, 0:1, :] for k in range(layers)], axis=1)
    near_slots = jnp.concatenate([meta[upper + k, 1, 0:1, :] for k in range(layers)], axis=1)
    near_mine = (near_targets >= first) & (near_targets < first + ao_dev)
    near_slots = jnp.where(near_mine, near_slots - upper * slots_of, -1)
    near_select = one_hot(LANES, near_slots)
    near_labels = label_row(jnp.where(near_mine, near_targets - first + 1, 0), near_select)
    near_owned = times(near_select, near).astype(jnp.bfloat16)
    for offset in range(naux - 1, -1, -1):
        fitted = times(one_hot(cols, near_targets - mirrored(column, offset) * cols), near).astype(jnp.bfloat16)
        near_fitted[offset] = fitted
        sent_near[offset, :near_rows] = crossed(near_owned, fitted)[:near_rows]
        sent_near[offset, near_rows:] = near_labels
        if offset:
            ship_near(offset).start()

    gather_step(npair - 1)

    last = held[far]
    far_targets = meta[far, 0, 0:1, :]
    far_ranks = meta[far, 1, 0:1, :] - far * slots_of
    far_mine = (far_targets >= first) & (far_targets < first + ao_dev)
    far_select = one_hot(slots_of, jnp.where(far_mine, far_ranks, -1))
    far_select_wide = one_hot(LANES, jnp.where(far_mine, far_ranks, -1))
    far_labels = label_row(jnp.where(far_mine, far_targets - first + 1, 0), far_select_wide)
    far_owned = times(far_select, last).astype(jnp.bfloat16)
    top_row = lax.broadcasted_iota(jnp.int32, (LABEL_ROWS, LANES), 0) == 0
    for offset in range(naux - 1, -1, -1):
        shifted = far_targets - mirrored(column, offset) * cols
        inside = (shifted >= 0) & (shifted < cols)
        ranks = jnp.where(inside, far_ranks, -1)
        moved = times(one_hot(slots_of, ranks), last).astype(jnp.bfloat16)
        column_labels = label_row(jnp.where(inside, shifted + 1, 0), one_hot(LANES, ranks))
        fitted = times(one_hot(cols, shifted), last).astype(jnp.bfloat16)
        sent_far[offset, :slots_of] = crossed(far_owned, near_fitted[offset]) + crossed(far_owned, fitted)
        sent_far[offset, slots_of:2 * slots_of] = crossed(moved, near_owned)
        sent_far[offset, 2 * slots_of:] = jnp.where(top_row, far_labels, column_labels)
        if offset:
            ship_far(offset).start()

    def split(value):
        high = value.astype(jnp.bfloat16)
        return high, (value - high.astype(jnp.float32)).astype(jnp.bfloat16)

    def spread(count, label):
        row = (lax.broadcasted_iota(jnp.int32, (count, label.shape[1]), 0) + 1).astype(jnp.float32)
        return (row == label).astype(jnp.float32).astype(jnp.bfloat16)

    total = jnp.zeros((ao_dev, cols), jnp.float32)
    for offset in range(naux):
        if offset:
            ship_near(offset).wait_recv()
        source = near_in if offset else sent_near
        rows_near = spread(ao_dev, source[offset, near_rows:near_rows + 1, :])
        high, low = split(source[offset, :near_rows])
        total = total + times(rows_near[:, :near_rows], high) + times(rows_near[:, :near_rows], low)
    for offset in range(naux):
        if offset:
            ship_far(offset).wait_recv()
        near_source = near_in if offset else sent_near
        source = far_in if offset else sent_far
        rows_near = spread(ao_dev, near_source[offset, near_rows:near_rows + 1, :])
        rows_far = spread(ao_dev, source[offset, 2 * slots_of:2 * slots_of + 1, :slots_of])
        cols_far = spread(cols, source[offset, 2 * slots_of + 1:2 * slots_of + 2, :slots_of])
        high, low = split(source[offset, :slots_of])
        total = total + times(rows_far, high) + times(rows_far, low)
        high, low = split(source[offset, slots_of:2 * slots_of])
        high, low = split(times(cols_far, high) + times(cols_far, low))
        total = total + crossed(rows_near, high) + crossed(rows_near, low)
    out_ref[...] = total

    for offset in range(1, naux):
        ship_near(offset).wait_send()
        ship_far(offset).wait_send()
    for layer in range(npair):
        for part in range(parts):

            @pl.when((here < npair - 1) & (here >= layer))
            def _():
                move(layer, part, 1).wait_send()
                if part == parts - 1:
                    move_meta(layer, 1).wait_send()

            @pl.when((here > 0) & (here <= layer))
            def _():
                move(layer, part, -1).wait_send()
                if part == parts - 1:
                    move_meta(layer, -1).wait_send()


def fused(integrals, mu_list, lam_list, coeffs, block_size, block_order):
    tiles, aux_rows, width, _ = integrals.shape
    nblk, _, nocc = coeffs.shape
    npair = lax.axis_size("pair")
    naux = lax.axis_size("aux")
    ao_dev = nblk // npair * width
    cols = nblk * width // naux
    near_rows = (npair - 1) * CAP * width + LABEL_ROWS
    far_rows = 2 * CAP * width + LABEL_ROWS
    vmem = pl.BlockSpec(memory_space=pltpu.VMEM)
    dma = pltpu.SemaphoreType.DMA
    hbm = pl.BlockSpec(memory_space=pltpu.HBM)
    parts = 3 if tiles % 3 == 0 else 1
    return pl.pallas_call(
        functools.partial(exchange_kernel, npair, naux, parts),
        out_shape=jax.ShapeDtypeStruct((ao_dev, cols), jnp.float32),
        in_specs=[hbm] * 6,
        out_specs=vmem,
        scratch_shapes=[
            pltpu.SMEM(mu_list.shape, jnp.int32),
            pltpu.SMEM((tiles, 1, lam_list.shape[2]), jnp.int32),
            pltpu.SMEM(block_size.shape, jnp.int32),
            pltpu.SMEM(block_order.shape, jnp.int32),
            dma((4,)),
            pltpu.VMEM(integrals.shape, jnp.float32),
            pltpu.VMEM(coeffs.shape, jnp.float32),
            dma((parts + 1,)),
            pltpu.VMEM((npair, LANES, aux_rows * nocc), jnp.bfloat16),
            pltpu.VMEM((npair, 2, LABEL_ROWS, LANES), jnp.int32),
            pltpu.VMEM((naux, cols, aux_rows * nocc), jnp.bfloat16),
            pltpu.VMEM((naux, near_rows, cols), jnp.float32),
            pltpu.VMEM((naux, near_rows, cols), jnp.float32),
            pltpu.VMEM((naux, far_rows, cols), jnp.float32),
            pltpu.VMEM((naux, far_rows, cols), jnp.float32),
            dma((npair, parts)), dma((npair, parts)), dma((npair, parts)),
            dma((npair,)), dma((npair,)), dma((npair,)),
            dma((naux,)), dma((naux,)), dma((naux,)), dma((naux,)),
        ],
        compiler_params=pltpu.CompilerParams(
            collective_id=0, has_side_effects=True, vmem_limit_bytes=60 * 1024 * 1024
        ),
    )(mu_list, jnp.transpose(lam_list, (1, 0, 2)), block_size, block_order, integrals, coeffs)


def fits(integrals, mu_list, lam_list, coeffs, block_size, block_order):
    tiles, aux_rows, width, depth = integrals.shape
    nblk, _, nocc = coeffs.shape
    npair = lax.axis_size("pair")
    naux = lax.axis_size("aux")
    return (
        tiles * width <= LANES
        and npair * CAP * width == LANES
        and nblk * width // naux == LANES
        and 2 * nocc == LANES
        and aux_rows % 2 == 0
        and width % 16 == 0
        and npair % 2 == 0
        and nblk // npair * width <= 256
        and naux & (naux - 1) == 0
    )


def device(*arrays):
    return fused(*arrays) if fits(*arrays) else body(*arrays)


def solution(mesh):
    return jax.shard_map(
        device,
        mesh=mesh,
        in_specs=(
            P("pair", "aux", None, None),
            P("aux", "pair"),
            P("aux", "pair", None),
            P(),
            P(),
            P(),
        ),
        out_specs=P("pair", "aux"),
        check_vma=False,
    )
```

```python
import functools

import jax
import jax.numpy as jnp
from jax import lax
from jax.experimental import pallas as pl
from jax.experimental.pallas import tpu as pltpu
from jax.sharding import PartitionSpec as P

CAP = 2
LANES = 128
LABEL_ROWS = 8
MESH = pl.DeviceIdType.MESH


def crossed(left, right):
    return lax.dot_general(
        left, right, (((1,), (1,)), ((), ())), preferred_element_type=jnp.float32
    )


def body(integrals, mu_list, lam_list, coeffs, block_size, block_order):
    tiles = integrals.shape[0]
    aux_rows = integrals.shape[1]
    width = integrals.shape[2]
    nblk, _, nocc = coeffs.shape
    npair = lax.axis_size("pair")
    here = lax.axis_index("pair")
    blk_dev = nblk // npair
    ao_dev = blk_dev * width
    slot_count = npair * CAP
    span = jnp.arange(width, dtype=jnp.int32)
    live = (span[None, :] < block_size[:, None]).astype(jnp.float32)
    masked = coeffs * live[:, :, None]
    picked = masked[lam_list[0]].reshape(tiles, -1, nocc)
    half = jnp.einsum("tqmk,tki->tmqi", integrals, picked, precision=lax.Precision.HIGHEST)
    half = half.astype(jnp.bfloat16).reshape(tiles, width * aux_rows * nocc)
    place = block_order[mu_list[0]]
    owner = place // blk_dev
    local = place % blk_dev
    order_ids = jnp.arange(tiles, dtype=jnp.int32)
    earlier = (owner[None, :] == owner[:, None]) & (order_ids[None, :] < order_ids[:, None])
    rank = jnp.sum(earlier.astype(jnp.int32), axis=1)
    slot = owner * CAP + rank
    select = jnp.arange(slot_count, dtype=jnp.int32)[:, None] == slot[None, :]
    outgoing = jnp.dot(
        select.astype(jnp.bfloat16), half, preferred_element_type=jnp.float32
    ).astype(jnp.bfloat16)
    outgoing = outgoing.reshape(npair, CAP, width * aux_rows * nocc)
    labels = jnp.sum(jnp.where(select, local[None, :] + 1, 0), axis=1) - 1
    labels = labels.reshape(npair, CAP)
    incoming, labels_in = (
        lax.all_to_all(outgoing, "pair", split_axis=0, concat_axis=0, tiled=True),
        lax.all_to_all(labels, "pair", split_axis=0, concat_axis=0, tiled=True),
    )
    assign = (
        labels_in.reshape(-1)[None, :] == jnp.arange(blk_dev, dtype=jnp.int32)[:, None]
    ).astype(jnp.bfloat16)
    fitted = jnp.dot(assign, incoming.reshape(slot_count, -1), preferred_element_type=jnp.float32)
    fitted = fitted.astype(jnp.bfloat16).reshape(ao_dev, aux_rows * nocc)
    partial_value = crossed(fitted, lax.all_gather(fitted, "pair", axis=0, tiled=True))
    summed = lax.psum_scatter(partial_value, "aux", scatter_dimension=1, tiled=True)
    posmat = (block_order[None, :] == jnp.arange(nblk, dtype=jnp.int32)[:, None]).astype(
        jnp.float32
    )
    live_pos = jnp.dot(posmat, live, precision=lax.Precision.HIGHEST).reshape(-1)
    cols = summed.shape[1]
    row_mask = lax.dynamic_slice_in_dim(live_pos, here * ao_dev, ao_dev, 0)
    col_mask = lax.dynamic_slice_in_dim(live_pos, lax.axis_index("aux") * cols, cols, 0)
    return summed * row_mask[:, None] * col_mask[None, :]


def mirrored(index, offset):
    result = index
    bit = 1
    while bit <= offset:
        if offset & bit:
            result = result + bit * (1 - 2 * ((index // bit) % 2))
        bit *= 2
    return result


def exchange_kernel(
    npair, naux, parts, mu_hbm, lam_hbm, size_hbm, order_hbm, integrals_hbm, coeffs_hbm, out_ref,
    mu_ref, lam_ref, size_ref, order_ref, scalar_sem, integrals_ref, coeffs_ref, load_sem, held, meta, near_fitted, sent_near, near_in, sent_far, far_in, out_left, out_right, in_sem, meta_left, meta_right, meta_in,
    near_out, near_arrived, far_out, far_arrived,
):
    tiles, aux_rows, width, depth = integrals_ref.shape
    nocc = coeffs_ref.shape[2]
    partners = depth // width
    ao_dev, cols = out_ref.shape
    rows = tiles * width
    padded = held.shape[1]
    chunk = rows // parts
    group = tiles // parts
    here = lax.axis_index("pair")
    column = lax.axis_index("aux")
    low_layer = here < npair // 2
    high_layer = here >= npair // 2

    scalar_loads = []
    for source, dest in ((mu_hbm, mu_ref), (lam_hbm, lam_ref), (size_hbm, size_ref), (order_hbm, order_ref)):
        scalar_loads.append(pltpu.make_async_copy(source, dest, scalar_sem.at[len(scalar_loads)]))
        scalar_loads[-1].start()
    coeffs_load = pltpu.make_async_copy(coeffs_hbm, coeffs_ref, load_sem.at[parts])
    coeffs_load.start()
    loads = []
    for part in range(parts):
        wanted = pl.ds(part * group, group)
        loads.append(pltpu.make_async_copy(integrals_hbm.at[wanted], integrals_ref.at[wanted], load_sem.at[part]))
        loads[part].start()

    barrier = pltpu.get_barrier_semaphore()

    def greet(device):
        pl.semaphore_signal(barrier, inc=1, device_id=device, device_id_type=MESH)

    for offset in range(1, naux):
        greet({"aux": mirrored(column, offset)})

    @pl.when(here > 0)
    def _():
        greet({"pair": here - 1})

    @pl.when(here < npair - 1)
    def _():
        greet({"pair": here + 1})

    for load in scalar_loads:
        load.wait()
    lane = lax.broadcasted_iota(jnp.int32, (LABEL_ROWS, LANES), 1)
    places = [order_ref[mu_ref[0, t]] for t in range(tiles)]
    target = jnp.full((LABEL_ROWS, LANES), -1, jnp.int32)
    slots = jnp.full((LABEL_ROWS, LANES), -1, jnp.int32)
    for t in range(tiles):
        rank = jnp.int32(0)
        for u in range(t):
            rank = rank + (places[u] // (ao_dev // width) == places[t] // (ao_dev // width)).astype(jnp.int32)
        mine = (lane >= t * width) & (lane < (t + 1) * width)
        within = lane - t * width
        target = jnp.where(mine, places[t] * width + within, target)
        slots = jnp.where(mine, (here * CAP + rank) * width + within, slots)
    meta[here, 0] = target
    meta[here, 1] = slots

    if padded > rows:
        for layer in range(npair):
            held[layer, rows:padded, :] = jnp.zeros((padded - rows, held.shape[2]), held.dtype)

    row_in_block = lax.broadcasted_iota(jnp.int32, (width, nocc), 0)
    packed = aux_rows // 2 * width
    low_half = lax.broadcasted_iota(jnp.int32, (packed, 2 * nocc), 1) < nocc
    row_in_tile = lax.broadcasted_iota(jnp.int32, (packed, 2 * nocc), 0) % width

    def transform(t):
        blocks = []
        for l in range(partners):
            block = lam_ref[t, 0, l]
            blocks.append(jnp.where(row_in_block < size_ref[block], coeffs_ref[block], 0.0))
        picked = jnp.concatenate(blocks, axis=0)
        picked = jnp.concatenate([picked, picked], axis=1)
        full = jnp.dot(
            integrals_ref[t].reshape(aux_rows * width, depth), picked,
            precision=lax.Precision.HIGHEST, preferred_element_type=jnp.float32,
        )
        half = jnp.where(low_half, full[:packed], full[packed:])
        half = jnp.where(row_in_tile < size_ref[mu_ref[0, t]], half, 0.0).astype(held.dtype)
        for j in range(aux_rows // 2):
            held[here, t * width:(t + 1) * width, j * 2 * nocc:(j + 1) * 2 * nocc] = half[j * width:(j + 1) * width]

    def move(layer, part, step):
        sem = (out_left if step < 0 else out_right).at[layer, part]
        piece = held.at[layer, pl.ds(part * chunk, chunk)]
        return pltpu.make_async_remote_copy(
            src_ref=piece, dst_ref=piece, send_sem=sem, recv_sem=in_sem.at[layer, part],
            device_id={"pair": here + step}, device_id_type=MESH,
        )

    def move_meta(layer, step):
        sem = (meta_left if step < 0 else meta_right).at[layer]
        return pltpu.make_async_remote_copy(
            src_ref=meta.at[layer], dst_ref=meta.at[layer], send_sem=sem, recv_sem=meta_in.at[layer],
            device_id={"pair": here + step}, device_id_type=MESH,
        )

    def push(layer, part, step):
        move(layer, part, step).start()
        if part == parts - 1:
            move_meta(layer, step).start()

    def take(layer, part, step):
        move(layer, part, step).wait_recv()
        if part == parts - 1:
            move_meta(layer, step).wait_recv()

    coeffs_load.wait()
    for part in range(parts):
        loads[part].wait()
        for t in range(part * group, (part + 1) * group):
            transform(t)
        if part == 0:
            before = (here + npair - 1) // npair
            after = (2 * npair - 2 - here) // npair
            pl.semaphore_wait(barrier, naux - 1 + before + after)

        @pl.when((here > 0) & low_layer)
        def _():
            push(here, part, -1)

        @pl.when(here < npair - 1)
        def _():
            push(here, part, 1)

        @pl.when((here > 0) & high_layer)
        def _():
            push(here, part, -1)

    def pass_on(hops, part, step):
        take(here + step * hops, part, step)
        onward = here > 0 if step > 0 else here < npair - 1

        @pl.when(onward)
        def _():
            push(here + step * hops, part, step * -1)

    def gather_step(hops):
        for part in range(parts):

            @pl.when((here + hops < npair) & low_layer)
            def _():
                pass_on(hops, part, 1)

            @pl.when(here >= hops)
            def _():
                pass_on(hops, part, -1)

            @pl.when((here + hops < npair) & high_layer)
            def _():
                pass_on(hops, part, 1)

    def one_hot(rows_of, wanted_row):
        found = lax.broadcasted_iota(jnp.int32, (rows_of, wanted_row.shape[1]), 0) == wanted_row
        return found.astype(jnp.float32).astype(jnp.bfloat16)

    def times(left, right):
        return jnp.dot(left, right, preferred_element_type=jnp.float32)

    def label_row(local, select):
        local = jnp.broadcast_to(local.astype(jnp.float32), (16, local.shape[1])).astype(jnp.bfloat16)
        return crossed(local, select)[:LABEL_ROWS]

    def split(value):
        high = value.astype(jnp.bfloat16)
        return high, (value - high.astype(jnp.float32)).astype(jnp.bfloat16)

    def ship(source, dest, out_sems, in_sems, offset):
        return pltpu.make_async_remote_copy(
            src_ref=source.at[offset], dst_ref=dest.at[offset],
            send_sem=out_sems.at[offset], recv_sem=in_sems.at[offset],
            device_id={"aux": mirrored(column, offset)}, device_id_type=MESH,
        )

    def ship_near(offset):
        return ship(sent_near, near_in, near_out, near_arrived, offset)

    def ship_far(offset):
        return ship(sent_far, far_in, far_out, far_arrived, offset)

    for hops in range(1, npair - 1):
        gather_step(hops)

    upper = here // (npair // 2)
    far = (npair - 1) * (1 - upper)
    layers = npair - 1
    slots_of = CAP * width
    near_rows = layers * slots_of
    first = here * ao_dev

    near = held[pl.ds(upper, layers)].reshape(layers * padded, held.shape[2])
    near_targets = jnp.concatenate([meta[upper + k, 0, 0:1, :] for k in range(layers)], axis=1)
    near_slots = jnp.concatenate([meta[upper + k, 1, 0:1, :] for k in range(layers)], axis=1)
    near_mine = (near_targets >= first) & (near_targets < first + ao_dev)
    near_slots = jnp.where(near_mine, near_slots - upper * slots_of, -1)
    near_select = one_hot(LANES, near_slots)
    near_labels = label_row(jnp.where(near_mine, near_targets - first + 1, 0), near_select)
    near_owned = times(near_select, near).astype(jnp.bfloat16)
    for offset in range(naux - 1, -1, -1):
        fitted = times(one_hot(cols, near_targets - mirrored(column, offset) * cols), near).astype(jnp.bfloat16)
        near_fitted[offset] = fitted
        sent_near[offset, :near_rows] = crossed(near_owned, fitted)[:near_rows]
        sent_near[offset, near_rows:] = near_labels
        if offset:
            ship_near(offset).start()

    gather_step(npair - 1)

    last = held[far]
    far_targets = meta[far, 0, 0:1, :]
    far_ranks = meta[far, 1, 0:1, :] - far * slots_of
    far_mine = (far_targets >= first) & (far_targets < first + ao_dev)
    far_select = one_hot(slots_of, jnp.where(far_mine, far_ranks, -1))
    far_select_wide = one_hot(LANES, jnp.where(far_mine, far_ranks, -1))
    far_labels = label_row(jnp.where(far_mine, far_targets - first + 1, 0), far_select_wide)
    far_owned = times(far_select, last).astype(jnp.bfloat16)
    own_high, own_low = split(crossed(far_owned, last))
    far_high, far_low = split(crossed(last, near_owned))
    top_row = lax.broadcasted_iota(jnp.int32, (LABEL_ROWS, LANES), 0) == 0
    for offset in range(naux - 1, -1, -1):
        shifted = far_targets - mirrored(column, offset) * cols
        inside = (shifted >= 0) & (shifted < cols)
        ranks = jnp.where(inside, far_ranks, -1)
        column_labels = label_row(jnp.where(inside, shifted + 1, 0), one_hot(LANES, ranks))
        moved = one_hot(slots_of, ranks)
        spot = one_hot(cols, shifted)
        sent_far[offset, :slots_of] = (
            crossed(far_owned, near_fitted[offset]) + crossed(own_high, spot) + crossed(own_low, spot)
        )
        sent_far[offset, slots_of:2 * slots_of] = times(moved, far_high) + times(moved, far_low)
        sent_far[offset, 2 * slots_of:] = jnp.where(top_row, far_labels, column_labels)
        if offset:
            ship_far(offset).start()

    def spread(count, label):
        row = (lax.broadcasted_iota(jnp.int32, (count, label.shape[1]), 0) + 1).astype(jnp.float32)
        return (row == label).astype(jnp.float32).astype(jnp.bfloat16)

    total = jnp.zeros((ao_dev, cols), jnp.float32)
    for offset in range(naux):
        if offset:
            ship_near(offset).wait_recv()
        source = near_in if offset else sent_near
        rows_near = spread(ao_dev, source[offset, near_rows:near_rows + 1, :])
        high, low = split(source[offset, :near_rows])
        total = total + times(rows_near[:, :near_rows], high) + times(rows_near[:, :near_rows], low)
    for offset in range(naux):
        if offset:
            ship_far(offset).wait_recv()
        near_source = near_in if offset else sent_near
        source = far_in if offset else sent_far
        rows_near = spread(ao_dev, near_source[offset, near_rows:near_rows + 1, :])
        rows_far = spread(ao_dev, source[offset, 2 * slots_of:2 * slots_of + 1, :slots_of])
        cols_far = spread(cols, source[offset, 2 * slots_of + 1:2 * slots_of + 2, :slots_of])
        high, low = split(source[offset, :slots_of])
        total = total + times(rows_far, high) + times(rows_far, low)
        high, low = split(source[offset, slots_of:2 * slots_of])
        high, low = split(times(cols_far, high) + times(cols_far, low))
        total = total + crossed(rows_near, high) + crossed(rows_near, low)
    out_ref[...] = total

    for offset in range(1, naux):
        ship_near(offset).wait_send()
        ship_far(offset).wait_send()
    for layer in range(npair):
        for part in range(parts):

            @pl.when((here < npair - 1) & (here >= layer))
            def _():
                move(layer, part, 1).wait_send()
                if part == parts - 1:
                    move_meta(layer, 1).wait_send()

            @pl.when((here > 0) & (here <= layer))
            def _():
                move(layer, part, -1).wait_send()
                if part == parts - 1:
                    move_meta(layer, -1).wait_send()


def fused(integrals, mu_list, lam_list, coeffs, block_size, block_order):
    tiles, aux_rows, width, _ = integrals.shape
    nblk, _, nocc = coeffs.shape
    npair = lax.axis_size("pair")
    naux = lax.axis_size("aux")
    ao_dev = nblk // npair * width
    cols = nblk * width // naux
    near_rows = (npair - 1) * CAP * width + LABEL_ROWS
    far_rows = 2 * CAP * width + LABEL_ROWS
    vmem = pl.BlockSpec(memory_space=pltpu.VMEM)
    dma = pltpu.SemaphoreType.DMA
    hbm = pl.BlockSpec(memory_space=pltpu.HBM)
    parts = 3 if tiles % 3 == 0 else 1
    return pl.pallas_call(
        functools.partial(exchange_kernel, npair, naux, parts),
        out_shape=jax.ShapeDtypeStruct((ao_dev, cols), jnp.float32),
        in_specs=[hbm] * 6,
        out_specs=vmem,
        scratch_shapes=[
            pltpu.SMEM(mu_list.shape, jnp.int32),
            pltpu.SMEM((tiles, 1, lam_list.shape[2]), jnp.int32),
            pltpu.SMEM(block_size.shape, jnp.int32),
            pltpu.SMEM(block_order.shape, jnp.int32),
            dma((4,)),
            pltpu.VMEM(integrals.shape, jnp.float32),
            pltpu.VMEM(coeffs.shape, jnp.float32),
            dma((parts + 1,)),
            pltpu.VMEM((npair, LANES, aux_rows * nocc), jnp.bfloat16),
            pltpu.VMEM((npair, 2, LABEL_ROWS, LANES), jnp.int32),
            pltpu.VMEM((naux, cols, aux_rows * nocc), jnp.bfloat16),
            pltpu.VMEM((naux, near_rows, cols), jnp.float32),
            pltpu.VMEM((naux, near_rows, cols), jnp.float32),
            pltpu.VMEM((naux, far_rows, cols), jnp.float32),
            pltpu.VMEM((naux, far_rows, cols), jnp.float32),
            dma((npair, parts)), dma((npair, parts)), dma((npair, parts)),
            dma((npair,)), dma((npair,)), dma((npair,)),
            dma((naux,)), dma((naux,)), dma((naux,)), dma((naux,)),
        ],
        compiler_params=pltpu.CompilerParams(
            collective_id=0, has_side_effects=True, vmem_limit_bytes=60 * 1024 * 1024
        ),
    )(mu_list, jnp.transpose(lam_list, (1, 0, 2)), block_size, block_order, integrals, coeffs)


def fits(integrals, mu_list, lam_list, coeffs, block_size, block_order):
    tiles, aux_rows, width, depth = integrals.shape
    nblk, _, nocc = coeffs.shape
    npair = lax.axis_size("pair")
    naux = lax.axis_size("aux")
    return (
        tiles * width <= LANES
        and npair * CAP * width == LANES
        and nblk * width // naux == LANES
        and 2 * nocc == LANES
        and aux_rows % 2 == 0
        and width % 16 == 0
        and npair % 2 == 0
        and nblk // npair * width <= 256
        and naux & (naux - 1) == 0
    )


def device(*arrays):
    return fused(*arrays) if fits(*arrays) else body(*arrays)


def solution(mesh):
    return jax.shard_map(
        device,
        mesh=mesh,
        in_specs=(
            P("pair", "aux", None, None),
            P("aux", "pair"),
            P("aux", "pair", None),
            P(),
            P(),
            P(),
        ),
        out_specs=P("pair", "aux"),
        check_vma=False,
    )
```

```python
import functools

import jax
import jax.numpy as jnp
from jax import lax
from jax.experimental import pallas as pl
from jax.experimental.pallas import tpu as pltpu
from jax.sharding import PartitionSpec as P

CAP = 2
LANES = 128
LABEL_ROWS = 8
MESH = pl.DeviceIdType.MESH


def crossed(left, right):
    return lax.dot_general(
        left, right, (((1,), (1,)), ((), ())), preferred_element_type=jnp.float32
    )


def body(integrals, mu_list, lam_list, coeffs, block_size, block_order):
    tiles = integrals.shape[0]
    aux_rows = integrals.shape[1]
    width = integrals.shape[2]
    nblk, _, nocc = coeffs.shape
    npair = lax.axis_size("pair")
    here = lax.axis_index("pair")
    blk_dev = nblk // npair
    ao_dev = blk_dev * width
    slot_count = npair * CAP
    span = jnp.arange(width, dtype=jnp.int32)
    live = (span[None, :] < block_size[:, None]).astype(jnp.float32)
    masked = coeffs * live[:, :, None]
    picked = masked[lam_list[0]].reshape(tiles, -1, nocc)
    half = jnp.einsum("tqmk,tki->tmqi", integrals, picked, precision=lax.Precision.HIGHEST)
    half = half.astype(jnp.bfloat16).reshape(tiles, width * aux_rows * nocc)
    place = block_order[mu_list[0]]
    owner = place // blk_dev
    local = place % blk_dev
    order_ids = jnp.arange(tiles, dtype=jnp.int32)
    earlier = (owner[None, :] == owner[:, None]) & (order_ids[None, :] < order_ids[:, None])
    rank = jnp.sum(earlier.astype(jnp.int32), axis=1)
    slot = owner * CAP + rank
    select = jnp.arange(slot_count, dtype=jnp.int32)[:, None] == slot[None, :]
    outgoing = jnp.dot(
        select.astype(jnp.bfloat16), half, preferred_element_type=jnp.float32
    ).astype(jnp.bfloat16)
    outgoing = outgoing.reshape(npair, CAP, width * aux_rows * nocc)
    labels = jnp.sum(jnp.where(select, local[None, :] + 1, 0), axis=1) - 1
    labels = labels.reshape(npair, CAP)
    incoming, labels_in = (
        lax.all_to_all(outgoing, "pair", split_axis=0, concat_axis=0, tiled=True),
        lax.all_to_all(labels, "pair", split_axis=0, concat_axis=0, tiled=True),
    )
    assign = (
        labels_in.reshape(-1)[None, :] == jnp.arange(blk_dev, dtype=jnp.int32)[:, None]
    ).astype(jnp.bfloat16)
    fitted = jnp.dot(assign, incoming.reshape(slot_count, -1), preferred_element_type=jnp.float32)
    fitted = fitted.astype(jnp.bfloat16).reshape(ao_dev, aux_rows * nocc)
    partial_value = crossed(fitted, lax.all_gather(fitted, "pair", axis=0, tiled=True))
    summed = lax.psum_scatter(partial_value, "aux", scatter_dimension=1, tiled=True)
    posmat = (block_order[None, :] == jnp.arange(nblk, dtype=jnp.int32)[:, None]).astype(
        jnp.float32
    )
    live_pos = jnp.dot(posmat, live, precision=lax.Precision.HIGHEST).reshape(-1)
    cols = summed.shape[1]
    row_mask = lax.dynamic_slice_in_dim(live_pos, here * ao_dev, ao_dev, 0)
    col_mask = lax.dynamic_slice_in_dim(live_pos, lax.axis_index("aux") * cols, cols, 0)
    return summed * row_mask[:, None] * col_mask[None, :]


def mirrored(index, offset):
    result = index
    bit = 1
    while bit <= offset:
        if offset & bit:
            result = result + bit * (1 - 2 * ((index // bit) % 2))
        bit *= 2
    return result


def exchange_kernel(
    npair, naux, parts, mu_hbm, lam_hbm, size_hbm, order_hbm, integrals_hbm, coeffs_hbm, out_ref,
    mu_ref, lam_ref, size_ref, order_ref, scalar_sem, integrals_ref, coeffs_ref, load_sem, held, meta, near_fitted, sent_near, near_in, sent_far, far_in, out_left, out_right, in_sem, meta_left, meta_right, meta_in,
    near_out, near_arrived, far_out, far_arrived,
):
    tiles, aux_rows, width, depth = integrals_ref.shape
    nocc = coeffs_ref.shape[2]
    partners = depth // width
    ao_dev, cols = out_ref.shape
    rows = tiles * width
    padded = held.shape[1]
    chunk = rows // parts
    group = tiles // parts
    here = lax.axis_index("pair")
    column = lax.axis_index("aux")
    low_layer = here < npair // 2
    high_layer = here >= npair // 2

    scalar_loads = []
    for source, dest in ((mu_hbm, mu_ref), (lam_hbm, lam_ref), (size_hbm, size_ref), (order_hbm, order_ref)):
        scalar_loads.append(pltpu.make_async_copy(source, dest, scalar_sem.at[len(scalar_loads)]))
        scalar_loads[-1].start()
    coeffs_load = pltpu.make_async_copy(coeffs_hbm, coeffs_ref, load_sem.at[parts])
    coeffs_load.start()
    loads = []
    for part in range(parts):
        wanted = pl.ds(part * group, group)
        loads.append(pltpu.make_async_copy(integrals_hbm.at[wanted], integrals_ref.at[wanted], load_sem.at[part]))
        loads[part].start()

    barrier = pltpu.get_barrier_semaphore()

    def greet(device):
        pl.semaphore_signal(barrier, inc=1, device_id=device, device_id_type=MESH)

    for offset in range(1, naux):
        greet({"aux": mirrored(column, offset)})

    @pl.when(here > 0)
    def _():
        greet({"pair": here - 1})

    @pl.when(here < npair - 1)
    def _():
        greet({"pair": here + 1})

    for load in scalar_loads:
        load.wait()
    lane = lax.broadcasted_iota(jnp.int32, (LABEL_ROWS, LANES), 1)
    places = [order_ref[mu_ref[0, t]] for t in range(tiles)]
    target = jnp.full((LABEL_ROWS, LANES), -1, jnp.int32)
    slots = jnp.full((LABEL_ROWS, LANES), -1, jnp.int32)
    for t in range(tiles):
        rank = jnp.int32(0)
        for u in range(t):
            rank = rank + (places[u] // (ao_dev // width) == places[t] // (ao_dev // width)).astype(jnp.int32)
        mine = (lane >= t * width) & (lane < (t + 1) * width)
        within = lane - t * width
        target = jnp.where(mine, places[t] * width + within, target)
        slots = jnp.where(mine, (here * CAP + rank) * width + within, slots)
    meta[here, 0] = target
    meta[here, 1] = slots

    if padded > rows:
        for layer in range(npair):
            held[layer, rows:padded, :] = jnp.zeros((padded - rows, held.shape[2]), held.dtype)

    row_in_block = lax.broadcasted_iota(jnp.int32, (width, nocc), 0)
    packed = aux_rows // 2 * width
    low_half = lax.broadcasted_iota(jnp.int32, (packed, 2 * nocc), 1) < nocc
    row_in_tile = lax.broadcasted_iota(jnp.int32, (packed, 2 * nocc), 0) % width

    def transform(t):
        blocks = []
        for l in range(partners):
            block = lam_ref[t, 0, l]
            blocks.append(jnp.where(row_in_block < size_ref[block], coeffs_ref[block], 0.0))
        picked = jnp.concatenate(blocks, axis=0)
        picked = jnp.concatenate([picked, picked], axis=1)
        full = jnp.dot(
            integrals_ref[t].reshape(aux_rows * width, depth), picked,
            precision=lax.Precision.HIGHEST, preferred_element_type=jnp.float32,
        )
        half = jnp.where(low_half, full[:packed], full[packed:])
        half = jnp.where(row_in_tile < size_ref[mu_ref[0, t]], half, 0.0).astype(held.dtype)
        for j in range(aux_rows // 2):
            held[here, t * width:(t + 1) * width, j * 2 * nocc:(j + 1) * 2 * nocc] = half[j * width:(j + 1) * width]

    def move(layer, part, step):
        sem = (out_left if step < 0 else out_right).at[layer, part]
        piece = held.at[layer, pl.ds(part * chunk, chunk)]
        return pltpu.make_async_remote_copy(
            src_ref=piece, dst_ref=piece, send_sem=sem, recv_sem=in_sem.at[layer, part],
            device_id={"pair": here + step}, device_id_type=MESH,
        )

    def move_meta(layer, step):
        sem = (meta_left if step < 0 else meta_right).at[layer]
        return pltpu.make_async_remote_copy(
            src_ref=meta.at[layer], dst_ref=meta.at[layer], send_sem=sem, recv_sem=meta_in.at[layer],
            device_id={"pair": here + step}, device_id_type=MESH,
        )

    def push(layer, part, step):
        move(layer, part, step).start()
        if part == parts - 1:
            move_meta(layer, step).start()

    def take(layer, part, step):
        move(layer, part, step).wait_recv()
        if part == parts - 1:
            move_meta(layer, step).wait_recv()

    coeffs_load.wait()
    for part in range(parts):
        loads[part].wait()
        for t in range(part * group, (part + 1) * group):
            transform(t)
        if part == 0:
            before = (here + npair - 1) // npair
            after = (2 * npair - 2 - here) // npair
            pl.semaphore_wait(barrier, naux - 1 + before + after)

        @pl.when((here > 0) & low_layer)
        def _():
            push(here, part, -1)

        @pl.when(here < npair - 1)
        def _():
            push(here, part, 1)

        @pl.when((here > 0) & high_layer)
        def _():
            push(here, part, -1)

    def pass_on(hops, part, step):
        take(here + step * hops, part, step)
        onward = here > 0 if step > 0 else here < npair - 1

        @pl.when(onward)
        def _():
            push(here + step * hops, part, step * -1)

    send_order = sorted(range(naux), key=lambda offset: (-(offset % 2), -offset))
    send_order = [offset for offset in send_order if offset] + [0]

    def gather_step(hops):
        for part in range(parts):

            @pl.when((here + hops < npair) & low_layer)
            def _():
                pass_on(hops, part, 1)

            @pl.when(here >= hops)
            def _():
                pass_on(hops, part, -1)

            @pl.when((here + hops < npair) & high_layer)
            def _():
                pass_on(hops, part, 1)

    def one_hot(rows_of, wanted_row):
        found = lax.broadcasted_iota(jnp.int32, (rows_of, wanted_row.shape[1]), 0) == wanted_row
        return found.astype(jnp.float32).astype(jnp.bfloat16)

    def times(left, right):
        return jnp.dot(left, right, preferred_element_type=jnp.float32)

    def label_row(local, select):
        local = jnp.broadcast_to(local.astype(jnp.float32), (16, local.shape[1])).astype(jnp.bfloat16)
        return crossed(local, select)[:LABEL_ROWS]

    def ship(source, dest, out_sems, in_sems, offset):
        return pltpu.make_async_remote_copy(
            src_ref=source.at[offset], dst_ref=dest.at[offset],
            send_sem=out_sems.at[offset], recv_sem=in_sems.at[offset],
            device_id={"aux": mirrored(column, offset)}, device_id_type=MESH,
        )

    def ship_near(offset):
        return ship(sent_near, near_in, near_out, near_arrived, offset)

    def ship_far(offset):
        return ship(sent_far, far_in, far_out, far_arrived, offset)

    for hops in range(1, npair - 1):
        gather_step(hops)

    upper = here // (npair // 2)
    far = (npair - 1) * (1 - upper)
    layers = npair - 1
    slots_of = CAP * width
    near_rows = layers * slots_of
    first = here * ao_dev

    near = held[pl.ds(upper, layers)].reshape(layers * padded, held.shape[2])
    near_targets = jnp.concatenate([meta[upper + k, 0, 0:1, :] for k in range(layers)], axis=1)
    near_slots = jnp.concatenate([meta[upper + k, 1, 0:1, :] for k in range(layers)], axis=1)
    near_mine = (near_targets >= first) & (near_targets < first + ao_dev)
    near_slots = jnp.where(near_mine, near_slots - upper * slots_of, -1)
    near_select = one_hot(LANES, near_slots)
    near_labels = label_row(jnp.where(near_mine, near_targets - first + 1, 0), near_select)
    near_owned = times(near_select, near).astype(jnp.bfloat16)
    for offset in send_order:
        fitted = times(one_hot(cols, near_targets - mirrored(column, offset) * cols), near).astype(jnp.bfloat16)
        near_fitted[offset] = fitted
        sent_near[offset, :near_rows] = crossed(near_owned, fitted)[:near_rows]
        sent_near[offset, near_rows:] = near_labels
        if offset:
            ship_near(offset).start()

    gather_step(npair - 1)

    last = held[far]
    far_targets = meta[far, 0, 0:1, :]
    far_ranks = meta[far, 1, 0:1, :] - far * slots_of
    far_mine = (far_targets >= first) & (far_targets < first + ao_dev)
    far_select = one_hot(slots_of, jnp.where(far_mine, far_ranks, -1))
    far_select_wide = one_hot(LANES, jnp.where(far_mine, far_ranks, -1))
    far_labels = label_row(jnp.where(far_mine, far_targets - first + 1, 0), far_select_wide)
    far_owned = times(far_select, last).astype(jnp.bfloat16)
    top_row = lax.broadcasted_iota(jnp.int32, (LABEL_ROWS, LANES), 0) == 0
    for offset in send_order:
        shifted = far_targets - mirrored(column, offset) * cols
        inside = (shifted >= 0) & (shifted < cols)
        ranks = jnp.where(inside, far_ranks, -1)
        moved = times(one_hot(slots_of, ranks), last).astype(jnp.bfloat16)
        column_labels = label_row(jnp.where(inside, shifted + 1, 0), one_hot(LANES, ranks))
        fitted = times(one_hot(cols, shifted), last).astype(jnp.bfloat16)
        sent_far[offset, :slots_of] = crossed(far_owned, near_fitted[offset]) + crossed(far_owned, fitted)
        sent_far[offset, slots_of:2 * slots_of] = crossed(moved, near_owned)
        sent_far[offset, 2 * slots_of:] = jnp.where(top_row, far_labels, column_labels)
        if offset:
            ship_far(offset).start()

    def split(value):
        high = value.astype(jnp.bfloat16)
        return high, (value - high.astype(jnp.float32)).astype(jnp.bfloat16)

    def spread(count, label):
        row = (lax.broadcasted_iota(jnp.int32, (count, label.shape[1]), 0) + 1).astype(jnp.float32)
        return (row == label).astype(jnp.float32).astype(jnp.bfloat16)

    total = jnp.zeros((ao_dev, cols), jnp.float32)
    for offset in range(naux):
        if offset:
            ship_near(offset).wait_recv()
        source = near_in if offset else sent_near
        rows_near = spread(ao_dev, source[offset, near_rows:near_rows + 1, :])
        high, low = split(source[offset, :near_rows])
        total = total + times(rows_near[:, :near_rows], high) + times(rows_near[:, :near_rows], low)
    for offset in range(naux):
        if offset:
            ship_far(offset).wait_recv()
        near_source = near_in if offset else sent_near
        source = far_in if offset else sent_far
        rows_near = spread(ao_dev, near_source[offset, near_rows:near_rows + 1, :])
        rows_far = spread(ao_dev, source[offset, 2 * slots_of:2 * slots_of + 1, :slots_of])
        cols_far = spread(cols, source[offset, 2 * slots_of + 1:2 * slots_of + 2, :slots_of])
        high, low = split(source[offset, :slots_of])
        total = total + times(rows_far, high) + times(rows_far, low)
        high, low = split(source[offset, slots_of:2 * slots_of])
        high, low = split(times(cols_far, high) + times(cols_far, low))
        total = total + crossed(rows_near, high) + crossed(rows_near, low)
    out_ref[...] = total

    for offset in range(1, naux):
        ship_near(offset).wait_send()
        ship_far(offset).wait_send()
    for layer in range(npair):
        for part in range(parts):

            @pl.when((here < npair - 1) & (here >= layer))
            def _():
                move(layer, part, 1).wait_send()
                if part == parts - 1:
                    move_meta(layer, 1).wait_send()

            @pl.when((here > 0) & (here <= layer))
            def _():
                move(layer, part, -1).wait_send()
                if part == parts - 1:
                    move_meta(layer, -1).wait_send()


def fused(integrals, mu_list, lam_list, coeffs, block_size, block_order):
    tiles, aux_rows, width, _ = integrals.shape
    nblk, _, nocc = coeffs.shape
    npair = lax.axis_size("pair")
    naux = lax.axis_size("aux")
    ao_dev = nblk // npair * width
    cols = nblk * width // naux
    near_rows = (npair - 1) * CAP * width + LABEL_ROWS
    far_rows = 2 * CAP * width + LABEL_ROWS
    vmem = pl.BlockSpec(memory_space=pltpu.VMEM)
    dma = pltpu.SemaphoreType.DMA
    hbm = pl.BlockSpec(memory_space=pltpu.HBM)
    parts = 3 if tiles % 3 == 0 else 1
    return pl.pallas_call(
        functools.partial(exchange_kernel, npair, naux, parts),
        out_shape=jax.ShapeDtypeStruct((ao_dev, cols), jnp.float32),
        in_specs=[hbm] * 6,
        out_specs=vmem,
        scratch_shapes=[
            pltpu.SMEM(mu_list.shape, jnp.int32),
            pltpu.SMEM((tiles, 1, lam_list.shape[2]), jnp.int32),
            pltpu.SMEM(block_size.shape, jnp.int32),
            pltpu.SMEM(block_order.shape, jnp.int32),
            dma((4,)),
            pltpu.VMEM(integrals.shape, jnp.float32),
            pltpu.VMEM(coeffs.shape, jnp.float32),
            dma((parts + 1,)),
            pltpu.VMEM((npair, LANES, aux_rows * nocc), jnp.bfloat16),
            pltpu.VMEM((npair, 2, LABEL_ROWS, LANES), jnp.int32),
            pltpu.VMEM((naux, cols, aux_rows * nocc), jnp.bfloat16),
            pltpu.VMEM((naux, near_rows, cols), jnp.float32),
            pltpu.VMEM((naux, near_rows, cols), jnp.float32),
            pltpu.VMEM((naux, far_rows, cols), jnp.float32),
            pltpu.VMEM((naux, far_rows, cols), jnp.float32),
            dma((npair, parts)), dma((npair, parts)), dma((npair, parts)),
            dma((npair,)), dma((npair,)), dma((npair,)),
            dma((naux,)), dma((naux,)), dma((naux,)), dma((naux,)),
        ],
        compiler_params=pltpu.CompilerParams(
            collective_id=0, has_side_effects=True, vmem_limit_bytes=60 * 1024 * 1024
        ),
    )(mu_list, jnp.transpose(lam_list, (1, 0, 2)), block_size, block_order, integrals, coeffs)


def fits(integrals, mu_list, lam_list, coeffs, block_size, block_order):
    tiles, aux_rows, width, depth = integrals.shape
    nblk, _, nocc = coeffs.shape
    npair = lax.axis_size("pair")
    naux = lax.axis_size("aux")
    return (
        tiles * width <= LANES
        and npair * CAP * width == LANES
        and nblk * width // naux == LANES
        and 2 * nocc == LANES
        and aux_rows % 2 == 0
        and width % 16 == 0
        and npair % 2 == 0
        and nblk // npair * width <= 256
        and naux & (naux - 1) == 0
    )


def device(*arrays):
    return fused(*arrays) if fits(*arrays) else body(*arrays)


def solution(mesh):
    return jax.shard_map(
        device,
        mesh=mesh,
        in_specs=(
            P("pair", "aux", None, None),
            P("aux", "pair"),
            P("aux", "pair", None),
            P(),
            P(),
            P(),
        ),
        out_specs=P("pair", "aux"),
        check_vma=False,
    )
```
